32 devices in a mesh: dp: 4 (over y, x), fsdp: 8 (over z, core).
Axes of the slice: x: 2, y: 2, z: 4, core: 2. Of those that a mesh axis runs over, the one named last changes fastest.
Arguments:
- tokens: bfloat16 [4096, 8192], P(('dp', 'fsdp')), may hold values from -6 to 6
- frozen_key_matrix: bfloat16 [8192, 512], P('fsdp'), may hold values from -0.0625 to 0.0625
- adapter_down_factor: float32 [24, 8192, 16], P('fsdp', 'dp'), may hold values from -0.0625 to 0.0625
- adapter_up_factor: float32 [24, 16, 512], P('fsdp', None, 'dp'), may hold values from -1.5 to 1.5
- key_norm_gain: float32 [128], replicated, may hold values from 0.1 to 1.9
- adapter_offset: int32 [4, 8], P('dp', 'fsdp'), may hold values from 0 to 2, as said below
- loss_row_count: int32 [4, 8], P('dp', 'fsdp'), may hold values from 32 to 128, as said below
- cotangent: bfloat16 [4096, 512], P(('dp', 'fsdp')), may hold values from -6 to 6
Outputs:
- keys: bfloat16 [4096, 512], P(('dp', 'fsdp'))
- input_grad: bfloat16 [4096, 8192], P(('dp', 'fsdp'))
- down_grad: float32 [24, 8192, 16], P('fsdp', 'dp')
- up_factor_gradient: float32 [24, 16, 512], P('fsdp', None, 'dp')
The draws below stay inside these ranges and needn't reach their ends.
Inputs may be any that keep to these rules, and one draw needn't show every extreme that they name: `adapter_offset`: in every column j, each offset 0 to 2 is named by at least one dp index. `loss_row_count`: some block has 128 live rows and some block 32.
All inputs are finite; a program needn't handle non-finite values.
Results may differ from the reference program's by a relative error of at most 0.0033.
Values may be sent and summed in bfloat16 or wider, within the bound.
No kernel may reach another device: no remote copies, remote signals or barrier semaphores. Data moves between devices by JAX's collectives and lax.ppermute only.
A program may use at most 64 MiB of HBM per device.

```python
import jax
import jax.numpy as jnp
from jax import lax

MODEL_WIDTH = 8192
HD = 128
ADAPTER_RANK = 16
BLOCK_ROWS = 128
ADP_DEV = 3
KEY_WINDOW_WIDTH = 512
ADAPTER_COUNT = 24
DATA_GROUPS = 4
SHARDS = 8
TOKENS = 4096
N_DP = 4
N_FSDP = 8


def draw_adapter_offset(key, part):
    first_key, second_key = jax.random.split(jax.random.fold_in(key, 11))
    picked = jax.random.randint(first_key, (DATA_GROUPS, SHARDS), 0, ADP_DEV * ADP_DEV)
    skewed = jnp.minimum(picked % ADP_DEV, picked // ADP_DEV)
    positions = jnp.arange(DATA_GROUPS, dtype=jnp.int32)[:, None]
    values = jnp.where(positions < ADP_DEV, jnp.broadcast_to(positions % ADP_DEV, (DATA_GROUPS, SHARDS)), skewed)
    scores = jax.random.randint(second_key, (DATA_GROUPS, SHARDS), 0, 2 ** 20) * DATA_GROUPS + positions
    order = jnp.argsort(scores, axis=0, stable=True)
    return jnp.take_along_axis(values, order, axis=0).astype(jnp.int32)


def draw_loss_row_count(key, part):
    first_key, second_key, third_key = jax.random.split(jax.random.fold_in(key, 23), 3)
    total = DATA_GROUPS * SHARDS
    values = jax.random.randint(first_key, (total,), BLOCK_ROWS // 4, BLOCK_ROWS + 1)
    high_pos = jax.random.randint(second_key, (), 0, total)
    low_pos = (high_pos + 1 + jax.random.randint(third_key, (), 0, total - 1)) % total
    index = jnp.arange(total, dtype=jnp.int32)
    values = jnp.where(index == high_pos, BLOCK_ROWS, values)
    values = jnp.where(index == low_pos, BLOCK_ROWS // 4, values)
    return values.reshape(DATA_GROUPS, SHARDS).astype(jnp.int32)


def steps_of(key, dims, pieces, least, largest):
    level, own = 1.0, jax.random.fold_in(key, 6)
    for position, shards_of in pieces:
        steps = jnp.exp(jax.random.uniform(jax.random.fold_in(own, position), (shards_of,), jnp.float32, least / len(pieces), largest / len(pieces)))
        level = level * jnp.repeat(steps, dims[position] // shards_of).reshape([-1 if axis == position else 1 for axis in range(len(dims))])
    return level


def normal_values(key, shape, spread, bound, pieces=(), held_as=jnp.bfloat16):
    factor_of = steps_of(key, shape, pieces, -0.22, 0.18) if pieces else 1.0
    values = jax.random.normal(key, shape, jnp.float32) * spread * factor_of
    return jnp.minimum(jnp.maximum(values, -bound), bound).astype(held_as)


def setup_inputs(seed: int = 0) -> dict:
    key_of = jax.random.split(jax.random.key(seed), 9)
    return {
        "tokens": normal_values(key_of[0], (TOKENS, MODEL_WIDTH), 1.0, 6.0, ((0, 32),)),
        "frozen_key_matrix": normal_values(key_of[1], (MODEL_WIDTH, KEY_WINDOW_WIDTH), MODEL_WIDTH ** -0.5, 0.0625, ((0, 8),)),
        "adapter_down_factor": normal_values(key_of[2], (ADAPTER_COUNT, MODEL_WIDTH, ADAPTER_RANK), MODEL_WIDTH ** -0.5, 0.0625, ((0, 8), (1, 4)), jnp.float32),
        "adapter_up_factor": normal_values(key_of[3], (ADAPTER_COUNT, ADAPTER_RANK, KEY_WINDOW_WIDTH), ADAPTER_RANK ** -0.5, 1.5, ((0, 8), (2, 4)), jnp.float32),
        "key_norm_gain": jnp.clip(1.0 + 0.18 * jax.random.normal(key_of[4], (HD,), jnp.float32), 0.1, 1.9),
        "adapter_offset": draw_adapter_offset(jax.random.fold_in(key_of[8], 71), 0),
        "loss_row_count": draw_loss_row_count(jax.random.fold_in(key_of[8], 71), 0),
        "cotangent": normal_values(key_of[7], (TOKENS, KEY_WINDOW_WIDTH), 2.0, 6.0, ((0, 32),)),
    }


adapter_scale = 2.0
norm_eps = 1e-06

def block_pass(block_tokens, weight, down_projection, up_projection, key_norm_gain, live_count, adapter_total, block_cot):
    row_count = block_tokens.shape[0]
    highest_precision = lax.Precision.HIGHEST
    tokens_float = block_tokens.astype(jnp.float32)
    frozen_output = jnp.dot(block_tokens, weight, preferred_element_type=jnp.float32)
    lowrank_output = jnp.dot(tokens_float, down_projection, precision=highest_precision)
    projected_keys = frozen_output + adapter_scale * jnp.dot(lowrank_output, up_projection, precision=highest_precision)
    shaped = projected_keys.reshape(row_count, -1, HD)
    mean_square = lax.optimization_barrier(jnp.mean(shaped * shaped, axis=-1, keepdims=True))
    inverse_rms = lax.rsqrt(mean_square + norm_eps)
    normed = shaped * inverse_rms
    keys = (normed * key_norm_gain).reshape(row_count, -1).astype(jnp.bfloat16)
    row_mask = (jnp.arange(row_count, dtype=jnp.int32) < live_count).astype(jnp.float32)
    row_grad = block_cot.astype(jnp.float32) * row_mask[:, None] * (row_count / adapter_total)
    scaled_grad = row_grad.reshape(normed.shape) * key_norm_gain
    along_norm = lax.optimization_barrier(jnp.mean(scaled_grad * normed, axis=-1, keepdims=True))
    prenorm_gradient = (inverse_rms * (scaled_grad - normed * along_norm)).reshape(row_count, -1)
    pre_grad_low = prenorm_gradient.astype(jnp.bfloat16)
    lowrank_gradient = adapter_scale * jnp.dot(prenorm_gradient, up_projection.T, precision=highest_precision)
    input_base = lax.dot_general(pre_grad_low, weight, (((1,), (1,)), ((), ())), preferred_element_type=jnp.float32)
    input_grad = (input_base + jnp.dot(lowrank_gradient, down_projection.T, precision=highest_precision)).astype(jnp.bfloat16)
    down_grad = lax.dot_general(tokens_float, lowrank_gradient, (((0,), (0,)), ((), ())), precision=highest_precision)
    up_factor_gradient = adapter_scale * lax.dot_general(lowrank_output, prenorm_gradient, (((0,), (0,)), ((), ())), precision=highest_precision)
    return (keys, input_grad, down_grad, up_factor_gradient)

def reference(tokens, frozen_key_matrix, adapter_down_factor, adapter_up_factor, key_norm_gain, adapter_offset, loss_row_count, cotangent):
    blocks = N_DP * N_FSDP
    owner = jnp.broadcast_to(jnp.arange(N_FSDP, dtype=jnp.int32)[None, :], (N_DP, N_FSDP))
    global_ids = (owner * ADP_DEV + adapter_offset).reshape(-1).astype(jnp.int32)
    live_flat = loss_row_count.reshape(-1).astype(jnp.int32)
    totals = jnp.zeros((ADAPTER_COUNT,), jnp.int32).at[global_ids].add(live_flat)
    block_totals = totals[global_ids].astype(jnp.float32)
    token_blocks = tokens.reshape(blocks, BLOCK_ROWS, MODEL_WIDTH)
    cot_blocks = cotangent.reshape(blocks, BLOCK_ROWS, KEY_WINDOW_WIDTH)

    def per_block(accumulated, block_items):
        down_acc, up_acc = accumulated
        block_tokens, block_cot, adapter_number, live_count, adapter_total = block_items
        down_projection = lax.dynamic_index_in_dim(adapter_down_factor, adapter_number, 0, keepdims=False)
        up_projection = lax.dynamic_index_in_dim(adapter_up_factor, adapter_number, 0, keepdims=False)
        keys, input_grad, down_grad, up_factor_gradient = block_pass(block_tokens, frozen_key_matrix, down_projection, up_projection, key_norm_gain, live_count, adapter_total, block_cot)
        down_acc = lax.dynamic_update_index_in_dim(down_acc, lax.dynamic_index_in_dim(down_acc, adapter_number, 0, keepdims=False) + down_grad, adapter_number, 0)
        up_acc = lax.dynamic_update_index_in_dim(up_acc, lax.dynamic_index_in_dim(up_acc, adapter_number, 0, keepdims=False) + up_factor_gradient, adapter_number, 0)
        return ((down_acc, up_acc), (keys, input_grad))
    initial_carry = (jnp.zeros(adapter_down_factor.shape, jnp.float32), jnp.zeros(adapter_up_factor.shape, jnp.float32))
    (down_acc, up_acc), (all_keys, all_grads) = lax.scan(per_block, initial_carry, (token_blocks, cot_blocks, global_ids, live_flat, block_totals))
    return (all_keys.reshape(TOKENS, KEY_WINDOW_WIDTH), all_grads.reshape(TOKENS, MODEL_WIDTH), down_acc, up_acc)
```

```python
import functools

import jax
import jax.numpy as jnp
from jax import lax
from jax.experimental import pallas as pl
from jax.experimental.pallas import tpu as pltpu
from jax.sharding import PartitionSpec as P

HD = 128
CORES = 2

adapter_scale = 2.0
norm_eps = 1e-06

F32 = jnp.float32
BF16 = jnp.bfloat16
HIGHEST = lax.Precision.HIGHEST
VMEM_LIMIT = 48 * 2**20

vmem = pl.BlockSpec(memory_space=pltpu.VMEM)
smem = pl.BlockSpec(memory_space=pltpu.SMEM)


def split_two(value):
    high = value.astype(BF16)
    low = (value - high.astype(F32)).astype(BF16)
    return high, low


def call(kernel, outs, ins, name, flops=0, moved=0):
    return pl.pallas_call(
        kernel,
        out_shape=[jax.ShapeDtypeStruct(shape, dtype) for shape, dtype in outs],
        in_specs=[spec for spec, _ in ins],
        out_specs=[vmem] * len(outs),
        compiler_params=pltpu.CompilerParams(vmem_limit_bytes=VMEM_LIMIT),
        cost_estimate=pl.CostEstimate(flops=flops, bytes_accessed=moved, transcendentals=0),
        name=name,
    )(*[value for _, value in ins])


def messages_kernel(slots, down, up, *outs):
    width = down.shape[2]
    for partner, out in enumerate(outs):
        slot = slots[partner]
        out[:, :width] = down[slot]
        out[:, width:] = up[slot]


def low_rank_kernel(place, tokens, *refs):
    parts = len(refs) - 4
    messages, (split, up, low_rank, added) = refs[:parts], refs[parts:]
    rank = messages[0].shape[0]
    up_width = up.shape[1] // parts
    down_width = tokens.shape[1] // parts
    for partner, message in enumerate(messages):
        part = place[0] ^ partner
        columns = pl.ds(pl.multiple_of(part * down_width, 128), down_width)
        high, low = split_two(message[:, :down_width])
        split[:rank, columns] = high
        split[rank:, columns] = low
        columns = pl.ds(pl.multiple_of(part * up_width, 128), up_width)
        up[:, columns] = message[:, down_width:]
    both = lax.dot_general(tokens[...], split[...], (((1,), (1,)), ((), ())), preferred_element_type=F32)
    low_rank[...] = both[:, :rank] + both[:, rank:]
    added[...] = adapter_scale * jnp.dot(low_rank[...], up[...], precision=HIGHEST, preferred_element_type=F32)


def column_of(place, piece, part_rows):
    shard = (place[1] ^ piece["z"]) * CORES + (place[2] ^ piece["core"])
    part = 0 if piece["dp"] is None else place[0] ^ piece["dp"]
    column = (shard * piece["parts"] + part) * part_rows + piece["offset"]
    return pl.multiple_of(column, 128)


def base_sum(place, tokens, total, buffers, pieces, part_rows):
    for piece in pieces:
        columns = pl.ds(column_of(place, piece, part_rows), piece["rows"])
        rows = pl.ds(piece["first"], piece["rows"])
        total = total + jnp.dot(tokens[:, columns], buffers[piece["buffer"]][rows, :], preferred_element_type=F32)
    return total


def base_kernel(pieces, part_rows, place, tokens, before, *refs):
    refs[-1][...] = base_sum(place, tokens, before[...], refs[:-1], pieces, part_rows)


def middle_kernel(pieces, part_rows, parts, place, scale, tokens, before, cotangent, gain, low_rank, up, *refs):
    count = len(refs) - 3 - parts
    buffers, (keys, pre_low, low_grad), grads = refs[:count], refs[count : count + 3], refs[count + 3 :]
    projected = base_sum(place, tokens, before[...], buffers, pieces, part_rows)
    rows, width = projected.shape
    gains = gain[...]
    live = lax.broadcasted_iota(jnp.int32, (rows, 1), 0) < place[3]
    weight = jnp.where(live, scale[0], 0.0)
    heads = []
    for head in range(width // HD):
        columns = slice(head * HD, (head + 1) * HD)
        values = projected[:, columns]
        inverse = lax.rsqrt(jnp.mean(values * values, axis=-1, keepdims=True) + norm_eps)
        normed = values * inverse
        keys[:, columns] = (normed * gains).astype(BF16)
        scaled = cotangent[:, columns].astype(F32) * weight * gains
        along = jnp.mean(scaled * normed, axis=-1, keepdims=True)
        heads.append(inverse * (scaled - normed * along))
    pre = jnp.concatenate(heads, axis=-1)
    pre_low[...] = pre.astype(BF16)
    grad = adapter_scale * lax.dot_general(
        pre, up[...], (((1,), (1,)), ((), ())), precision=HIGHEST, preferred_element_type=F32
    )
    low_grad[...] = grad
    up_grad = adapter_scale * lax.dot_general(
        low_rank[...], pre, (((0,), (0,)), ((), ())), precision=HIGHEST, preferred_element_type=F32
    )
    rank = grad.shape[1]
    split = jnp.concatenate(split_two(grad), axis=-1)
    down_width, up_width = tokens.shape[1] // parts, width // parts
    for partner, out in enumerate(grads):
        part = place[0] ^ partner
        columns = pl.ds(pl.multiple_of(part * down_width, 128), down_width)
        both = lax.dot_general(split, tokens[:, columns], (((0,), (0,)), ((), ())), preferred_element_type=F32)
        out[:, :down_width] = (both[:rank] + both[rank:]).astype(out.dtype)
        for other in range(parts):

            @pl.when(part == other)
            def _():
                out[:, down_width:] = up_grad[:, other * up_width : (other + 1) * up_width].astype(out.dtype)


def input_grad_kernel(pieces, part_rows, place, pre_low, low_grad, split, *refs):
    buffers, out = refs[:-1], refs[-1]
    rank = low_grad.shape[1]
    high, low = split_two(low_grad[...])
    left = jnp.concatenate([high, high, low], axis=-1)
    for piece in pieces:
        columns = pl.ds(column_of(place, piece, part_rows), piece["rows"])
        rows = pl.ds(piece["first"], piece["rows"])
        value = lax.dot_general(
            pre_low[...], buffers[piece["buffer"]][rows, :], (((1,), (1,)), ((), ())), preferred_element_type=F32
        )
        right = jnp.concatenate([split[:, columns], split[:rank, columns]], axis=0)
        value = value + jnp.dot(left, right, preferred_element_type=F32)
        out[:, columns] = value.astype(BF16)


def sum_kernel(slots, *refs):
    grads, (down, up) = refs[:-2], refs[-2:]
    width = down.shape[2]
    for stored in range(down.shape[0]):
        total = jnp.zeros(grads[0].shape, F32)
        for partner, grad in enumerate(grads):
            total = total + jnp.where(slots[partner] == stored, grad[...].astype(F32), 0.0)
        down[stored] = total[:, :width]
        up[stored] = total[:, width:]


def flip(value, axis, size, bits):
    return lax.ppermute(value, axis, [(i, i ^ bits) for i in range(size)])


def on_device_lines(
    sizes,
    tokens,
    frozen_key_matrix,
    adapter_down_factor,
    adapter_up_factor,
    key_norm_gain,
    adapter_offset,
    loss_row_count,
    cotangent,
):
    parts, shards = sizes
    rows, model_width = tokens.shape
    key_width = frozen_key_matrix.shape[1]
    stored, down_width, rank = adapter_down_factor.shape
    up_width = adapter_up_factor.shape[2]
    shard_rows = frozen_key_matrix.shape[0]
    part_rows = shard_rows // parts
    half = part_rows // 2
    dp, fsdp = lax.axis_index("dp"), lax.axis_index("fsdp")
    over_dp = lambda value, bits: flip(value, "dp", parts, bits)
    over_z = lambda value, bits: flip(value, "fsdp", shards, bits * CORES)
    over_core = lambda value: flip(value, "fsdp", shards, 1)

    info = jnp.concatenate([adapter_offset[0], loss_row_count[0]])
    infos = [info] + [over_dp(info, bits) for bits in range(1, parts)]
    slots = jnp.stack([value[0] for value in infos])
    live = jnp.stack([value[1] for value in infos])
    adapter_total = jnp.sum(jnp.where(slots == slots[0], live, 0)).astype(F32)
    scale = (rows / adapter_total).reshape(1)
    place = jnp.stack([dp, fsdp // CORES, fsdp % CORES, info[1]]).astype(jnp.int32)

    message = ((rank, down_width + up_width), F32)
    messages = call(
        messages_kernel,
        [message] * parts,
        [(smem, slots), (vmem, jnp.swapaxes(adapter_down_factor, 1, 2)), (vmem, adapter_up_factor)],
        "adapter_messages",
    )
    adapters = [messages[0]] + [over_dp(messages[bits], bits) for bits in range(1, parts)]

    own = lax.dynamic_slice_in_dim(frozen_key_matrix, dp * part_rows, part_rows, 0)
    across = lax.dynamic_slice_in_dim(frozen_key_matrix, (dp ^ 3) * part_rows, part_rows, 0)
    z1 = over_z(own, 1)
    z2 = over_z(own, 2)
    z3 = over_z(z2, 1)
    d3 = over_z(across, 3)
    x1, y1 = over_dp(z1, 1), over_dp(z1, 2)
    x2 = over_dp(jnp.concatenate([z2, y1[half:]]), 1)
    y2 = over_dp(jnp.concatenate([z2, x1[:half]]), 2)
    x3 = over_dp(jnp.concatenate([z3, y2[half:part_rows]]), 1)
    y3 = over_dp(jnp.concatenate([z3, x2[:half]]), 2)

    def piece(z, dp_bits, count, first=0, offset=0):
        return dict(z=z, dp=dp_bits, rows=count, first=first, offset=offset, parts=parts)

    batches = [
        [(frozen_key_matrix, [piece(0, None, shard_rows)])],
        [
            (z1, [piece(1, 0, part_rows)]),
            (x1, [piece(1, 1, part_rows)]),
            (y1, [piece(1, 2, part_rows)]),
        ],
        [
            (z2, [piece(2, 0, part_rows)]),
            (x2, [piece(2, 1, part_rows), piece(1, 3, half, part_rows, half)]),
            (y2, [piece(2, 2, part_rows), piece(1, 3, half, part_rows, 0)]),
        ],
        [
            (z3, [piece(3, 0, part_rows)]),
            (d3, [piece(3, 3, part_rows)]),
            (x3, [piece(3, 1, part_rows), piece(2, 3, half, part_rows, half)]),
            (y3, [piece(3, 2, part_rows), piece(2, 3, half, part_rows, 0)]),
        ],
    ]
    batches = [
        [
            (value if core == 0 else over_core(value), [dict(item, core=core) for item in items])
            for value, items in batch
            for core in range(CORES)
        ]
        for batch in batches
    ]

    def flat(batch):
        buffers = [value for value, _ in batch]
        pieces = [dict(item, buffer=index) for index, (_, items) in enumerate(batch) for item in items]
        return buffers, pieces

    split, up, low_rank, total = call(
        low_rank_kernel,
        [((2 * rank, model_width), BF16), ((rank, key_width), F32), ((rows, rank), F32), ((rows, key_width), F32)],
        [(smem, place), (vmem, tokens)] + [(vmem, value) for value in adapters],
        "low_rank",
        flops=2 * rows * model_width * 256,
        moved=rows * model_width * 2,
    )
    for batch in batches[:-1]:
        buffers, pieces = flat(batch)
        (total,) = call(
            functools.partial(base_kernel, pieces, part_rows),
            [((rows, key_width), F32)],
            [(smem, place), (vmem, tokens), (vmem, total)] + [(vmem, value) for value in buffers],
            "base",
            flops=4 * rows * key_width * sum(item["rows"] for item in pieces),
            moved=sum(value.size for value in buffers) * 2,
        )
    buffers, pieces = flat(batches[-1])
    keys, pre_low, low_grad, *grads = call(
        functools.partial(middle_kernel, pieces, part_rows, parts),
        [((rows, key_width), BF16), ((rows, key_width), BF16), ((rows, rank), F32)] + [message] * parts,
        [
            (smem, place),
            (smem, scale),
            (vmem, tokens),
            (vmem, total),
            (vmem, cotangent),
            (vmem, key_norm_gain.reshape(1, HD)),
            (vmem, low_rank),
            (vmem, up),
        ]
        + [(vmem, value) for value in buffers],
        "key_norm",
        flops=4 * rows * key_width * model_width // 4,
        moved=sum(value.size for value in buffers) * 2,
    )
    received = [grads[0]] + [over_dp(grads[bits], bits) for bits in range(1, parts)]
    buffers, pieces = flat([entry for batch in batches for entry in batch])
    (input_grad,) = call(
        functools.partial(input_grad_kernel, pieces, part_rows),
        [((rows, model_width), BF16)],
        [(smem, place), (vmem, pre_low), (vmem, low_grad), (vmem, split)] + [(vmem, value) for value in buffers],
        "input_grad",
        flops=4 * rows * key_width * model_width,
        moved=2 * model_width * key_width,
    )
    down_sum, up_sum = call(
        sum_kernel,
        [((stored, rank, down_width), F32), ((stored, rank, up_width), F32)],
        [(smem, slots)] + [(vmem, value) for value in received],
        "grad_sum",
    )
    return keys, input_grad, jnp.swapaxes(down_sum, 1, 2), up_sum


def on_device_any(
    tokens,
    frozen_key_matrix,
    adapter_down_factor,
    adapter_up_factor,
    key_norm_gain,
    adapter_offset,
    loss_row_count,
    cotangent,
):
    row_count = tokens.shape[0]
    key_width = frozen_key_matrix.shape[1]
    stored_values = adapter_down_factor.shape[0]
    slot_value = adapter_offset[0, 0]
    live_count = loss_row_count[0, 0]
    selector = jnp.arange(stored_values, dtype=jnp.int32) == slot_value
    counted = jnp.where(selector, live_count, 0)
    summed_rows = lax.psum(counted, "dp")
    adapter_total = jnp.sum(jnp.where(selector, summed_rows, 0)).astype(F32)
    down_whole = lax.all_gather(adapter_down_factor, "dp", axis=1, tiled=True)
    up_whole = lax.all_gather(adapter_up_factor, "dp", axis=2, tiled=True)
    down_projection = lax.dynamic_index_in_dim(down_whole, slot_value, 0, keepdims=False)
    up_projection = lax.dynamic_index_in_dim(up_whole, slot_value, 0, keepdims=False)
    weight = lax.all_gather(frozen_key_matrix, "fsdp", axis=0, tiled=True)
    frozen_output = jnp.dot(tokens, weight, preferred_element_type=F32)
    tokens_float = tokens.astype(F32)
    lowrank_output = jnp.dot(tokens_float, down_projection, precision=HIGHEST)
    projected_keys = frozen_output + adapter_scale * jnp.dot(lowrank_output, up_projection, precision=HIGHEST)
    shaped = projected_keys.reshape(row_count, -1, HD)
    mean_square = jnp.mean(shaped * shaped, axis=-1, keepdims=True)
    inverse_rms = lax.rsqrt(mean_square + norm_eps)
    normed = shaped * inverse_rms
    keys = (normed * key_norm_gain).reshape(row_count, key_width).astype(BF16)
    row_mask = (jnp.arange(row_count, dtype=jnp.int32) < live_count).astype(F32)
    row_grad = cotangent.astype(F32) * row_mask[:, None] * (row_count / adapter_total)
    scaled_grad = row_grad.reshape(normed.shape) * key_norm_gain
    along_norm = jnp.mean(scaled_grad * normed, axis=-1, keepdims=True)
    prenorm_gradient = (inverse_rms * (scaled_grad - normed * along_norm)).reshape(row_count, key_width)
    pre_grad_low = prenorm_gradient.astype(BF16)
    lowrank_gradient = adapter_scale * jnp.dot(prenorm_gradient, up_projection.T, precision=HIGHEST)
    input_base = lax.dot_general(pre_grad_low, weight, (((1,), (1,)), ((), ())), preferred_element_type=F32)
    input_grad = (input_base + jnp.dot(lowrank_gradient, down_projection.T, precision=HIGHEST)).astype(BF16)
    down_grad = lax.dot_general(tokens_float, lowrank_gradient, (((0,), (0,)), ((), ())), precision=HIGHEST)
    up_factor_gradient = adapter_scale * lax.dot_general(
        lowrank_output, prenorm_gradient, (((0,), (0,)), ((), ())), precision=HIGHEST
    )
    selector_float = selector.astype(F32)
    down_terms = selector_float[:, None, None] * down_grad[None]
    up_terms = selector_float[:, None, None] * up_factor_gradient[None]
    down_sum = lax.psum_scatter(down_terms, "dp", scatter_dimension=1, tiled=True)
    up_sum = lax.psum_scatter(up_terms, "dp", scatter_dimension=2, tiled=True)
    return keys, input_grad, down_sum, up_sum


def solution(mesh):
    placed = (
        P(("dp", "fsdp"), None),
        P("fsdp", None),
        P("fsdp", "dp", None),
        P("fsdp", None, "dp"),
        P(),
        P("dp", "fsdp"),
        P("dp", "fsdp"),
        P(("dp", "fsdp"), None),
    )
    sizes = mesh.shape["dp"], mesh.shape["fsdp"]
    lines = sizes == (4, 4 * CORES)
    return jax.shard_map(
        functools.partial(on_device_lines, sizes) if lines else on_device_any,
        mesh=mesh,
        in_specs=placed,
        out_specs=(
            P(("dp", "fsdp"), None),
            P(("dp", "fsdp"), None),
            P("fsdp", "dp", None),
            P("fsdp", None, "dp"),
        ),
        check_vma=False,
    )
```

```python
import functools

import jax
import jax.numpy as jnp
from jax import lax
from jax.experimental import pallas as pl
from jax.experimental.pallas import tpu as pltpu
from jax.sharding import PartitionSpec as P

HD = 128
CORES = 2

adapter_scale = 2.0
norm_eps = 1e-06

F32 = jnp.float32
BF16 = jnp.bfloat16
HIGHEST = lax.Precision.HIGHEST
VMEM_LIMIT = 8 * 2**20

vmem = pl.BlockSpec(memory_space=pltpu.VMEM)
smem = pl.BlockSpec(memory_space=pltpu.SMEM)
hbm = pl.BlockSpec(memory_space=pltpu.HBM)


def split_two(value):
    high = value.astype(BF16)
    low = (value - high.astype(F32)).astype(BF16)
    return high, low


def call(kernel, outs, ins, name, scratch=(), limit=VMEM_LIMIT):
    return pl.pallas_call(
        kernel,
        out_shape=[jax.ShapeDtypeStruct(shape, dtype) for shape, dtype in outs],
        in_specs=[spec for spec, _ in ins],
        out_specs=[vmem] * len(outs),
        scratch_shapes=scratch,
        compiler_params=pltpu.CompilerParams(vmem_limit_bytes=limit),
        cost_estimate=pl.CostEstimate(flops=0, bytes_accessed=0, transcendentals=0),
        name=name,
    )(*[value for _, value in ins])


def position():
    fsdp = lax.axis_index("fsdp")
    return lax.axis_index("dp"), lax.div(fsdp, CORES), lax.rem(fsdp, CORES)


def start_kernel(matrix, near, far):
    rows = near.shape[0]
    parts = matrix.shape[0] // rows
    for out, bits in ((near, 0), (far, parts - 1)):
        part = lax.axis_index("dp") ^ bits
        out[...] = matrix[pl.ds(pl.multiple_of(part * rows, rows), rows), :]


def info_kernel(offset, info):
    info[...] = jnp.broadcast_to(offset[...].astype(F32), info.shape)


def hold_kernel(count, down, up, count_held, down_held, up_held):
    count_held[...] = jnp.broadcast_to(count[...].astype(F32), count_held.shape)
    down_held[...] = down[...]
    up_held[...] = up[...]


def chosen(stored, slot):
    return sum(jnp.where(slot == index, stored[index], 0.0) for index in range(stored.shape[0]))


def messages_kernel(*refs):
    parts = len(refs) - 7
    offsets, (count, down, up), (slots, own, sooner, later) = refs[:parts], refs[parts : parts + 3], refs[parts + 3 :]
    rank, width = down.shape[1], down.shape[2]
    wide = width + up.shape[2]
    first_core = position()[2] == 0
    for partner, offset in enumerate(offsets):
        slots[partner : partner + 1, :] = offset[...]
    near, side, beside, far = (offset[:, :1] for offset in offsets)
    wanted = jnp.where(first_core, side, beside), jnp.where(first_core, beside, side)
    for slot, out, first in ((near, own, 0), (wanted[0], sooner, 0), (wanted[1], later, 0), (far, sooner, rank)):
        rows = pl.ds(first, rank)
        out[rows, :width] = chosen(down, slot)
        out[rows, width:wide] = chosen(up, slot)
        out[rows, wide:] = jnp.broadcast_to(count[...], (rank, HD))


def pass_on_kernel(later, received, out):
    rank = later.shape[0]
    out[:rank] = later[...]
    out[rank:] = received[rank:]


def take_kernel(each, wanted, value, out):
    for index, place in enumerate(wanted):
        out[index * each : (index + 1) * each] = value[place * each : (place + 1) * each]


def join_kernel(each, *refs):
    out = refs[-1]
    for index, ref in enumerate(refs[:-1]):
        out[index * each : (index + 1) * each] = ref[:each]


def low_rank_kernel(tokens, slots, own, sooner, later, split, up, low_rank, total, told):
    rank = low_rank.shape[1]
    messages = own, sooner.at[:rank], later.at[:rank], later.at[rank:]
    parts = len(messages)
    down_width = tokens.shape[1] // parts
    up_width = up.shape[1] // parts
    dp, _, core = position()
    lane = lax.broadcasted_iota(jnp.int32, (1, HD), 1)
    counts = [message[:1, down_width + up_width :] for message in messages]
    counts[1:3] = jnp.where(core == 0, counts[1], counts[2]), jnp.where(core == 0, counts[2], counts[1])
    for partner, count in enumerate(counts):
        told[partner : partner + 1, :] = jnp.where(lane == 0, slots[partner : partner + 1, :], count)
    partners = 0, jnp.where(core == 0, 1, 2), jnp.where(core == 0, 2, 1), 3
    for partner, message in zip(partners, messages):
        part = dp ^ partner
        columns = pl.ds(pl.multiple_of(part * down_width, 128), down_width)
        high, low = split_two(message[:, :down_width])
        split[:rank, columns] = high
        split[rank:, columns] = low
        columns = pl.ds(pl.multiple_of(part * up_width, 128), up_width)
        up[:, columns] = message[:, down_width : down_width + up_width]
    both = lax.dot_general(tokens[...], split[...], (((1,), (1,)), ((), ())), preferred_element_type=F32)
    low_rank[...] = both[:, :rank] + both[:, rank:]
    total[...] = adapter_scale * jnp.dot(low_rank[...], up[...], precision=HIGHEST, preferred_element_type=F32)


def by_core(place, value):
    first, second = value
    return first if first == second else jnp.where(place[2] == 0, first, second)


def column_of(place, piece, part_rows, parts):
    shard = (place[1] ^ by_core(place, piece["z"])) * CORES + (place[2] ^ piece["core"])
    part = 0 if piece["dp"] is None else place[0] ^ by_core(place, piece["dp"])
    return pl.multiple_of((shard * parts + part) * part_rows, 128)


def base_sum(place, tokens, total, buffers, pieces, sizes):
    for piece in pieces:
        columns = pl.ds(column_of(place, piece, *sizes), piece["rows"])
        rows = pl.ds(piece["first"], piece["rows"])
        value = jnp.dot(tokens[:, columns], buffers[piece["buffer"]][rows, :], preferred_element_type=F32)
        total = value if total is None else total + value
    return total


def base_kernel(pieces, sizes, tokens, before, *refs):
    refs[-1][...] = base_sum(position(), tokens, before[...], refs[:-1], pieces, sizes)


def middle_kernel(pieces, sizes, told, *refs):
    parts = sizes[1]
    place = position()
    (tokens, before, cotangent, gain, low_rank, up), refs = refs[:6], refs[6:]
    count = len(refs) - 3 - parts
    buffers, (keys, pre_low, low_grad), grads = refs[:count], refs[count : count + 3], refs[count + 3 :]
    projected = base_sum(place, tokens, before[...], buffers, pieces, sizes)
    rows, width = projected.shape
    gains = gain[...]
    slots, counts = told[:, :1], told[:, 1:2]
    adapter_total = jnp.sum(jnp.where(slots == slots[:1], counts, 0.0), axis=0, keepdims=True)
    live = lax.broadcasted_iota(jnp.int32, (rows, 1), 0).astype(F32) < counts[:1]
    weight = rows / jnp.broadcast_to(adapter_total, (rows, 1))
    weight = jnp.where(live, weight, 0.0)
    heads = []
    for head in range(width // HD):
        columns = slice(head * HD, (head + 1) * HD)
        values = projected[:, columns]
        inverse = lax.rsqrt(jnp.mean(values * values, axis=-1, keepdims=True) + norm_eps)
        normed = values * inverse
        keys[:, columns] = (normed * gains).astype(BF16)
        scaled = cotangent[:, columns].astype(F32) * weight * gains
        along = jnp.mean(scaled * normed, axis=-1, keepdims=True)
        heads.append(inverse * (scaled - normed * along))
    pre = jnp.concatenate(heads, axis=-1)
    pre_low[...] = pre.astype(BF16)
    grad = adapter_scale * lax.dot_general(
        pre, up[...], (((1,), (1,)), ((), ())), precision=HIGHEST, preferred_element_type=F32
    )
    low_grad[...] = grad
    up_grad = adapter_scale * lax.dot_general(
        low_rank[...], pre, (((0,), (0,)), ((), ())), precision=HIGHEST, preferred_element_type=F32
    )
    rank = grad.shape[1]
    split = jnp.concatenate(split_two(grad), axis=-1)
    down_width, up_width = tokens.shape[1] // parts, width // parts
    for partner, out in enumerate(grads):
        part = place[0] ^ partner
        columns = pl.ds(pl.multiple_of(part * down_width, 128), down_width)
        both = lax.dot_general(split, tokens[:, columns], (((0,), (0,)), ((), ())), preferred_element_type=F32)
        out[:, :down_width] = (both[:rank] + both[rank:]).astype(out.dtype)
        for other in range(parts):

            @pl.when(part == other)
            def _():
                out[:, down_width:] = up_grad[:, other * up_width : (other + 1) * up_width].astype(out.dtype)


def input_grad_kernel(pieces, sizes, pre_low, low_grad, split, *refs):
    place = position()
    buffers, out = refs[:-1], refs[-1]
    rank = low_grad.shape[1]
    high, low = split_two(low_grad[...])
    left = jnp.concatenate([high, high, low], axis=-1)
    for piece in pieces:
        columns = pl.ds(column_of(place, piece, *sizes), piece["rows"])
        rows = pl.ds(piece["first"], piece["rows"])
        value = lax.dot_general(
            pre_low[...], buffers[piece["buffer"]][rows, :], (((1,), (1,)), ((), ())), preferred_element_type=F32
        )
        right = jnp.concatenate([split[:, columns], split[:rank, columns]], axis=0)
        value = value + jnp.dot(left, right, preferred_element_type=F32)
        out[:, columns] = value.astype(BF16)


def sum_kernel(told, *refs):
    grads, (down, up) = refs[:-2], refs[-2:]
    width = down.shape[2]
    for stored in range(down.shape[0]):
        total = jnp.zeros(grads[0].shape, F32)
        for partner, grad in enumerate(grads):
            slot = told[partner : partner + 1, :1]
            total = total + jnp.where(slot == stored, grad[...].astype(F32), 0.0)
        down[stored] = total[:, :width]
        up[stored] = total[:, width:]


def ordered(value, *earlier):
    return lax.optimization_barrier((value, *earlier))[0]


def flip(value, axis, size, bits):
    return lax.ppermute(value, axis, [(i, i ^ bits) for i in range(size)])


def on_device_lines(
    sizes,
    tokens,
    frozen_key_matrix,
    adapter_down_factor,
    adapter_up_factor,
    key_norm_gain,
    adapter_offset,
    loss_row_count,
    cotangent,
):
    parts, shards = sizes
    rows, model_width = tokens.shape
    key_width = frozen_key_matrix.shape[1]
    stored, down_width, rank = adapter_down_factor.shape
    up_width = adapter_up_factor.shape[2]
    shard_rows = frozen_key_matrix.shape[0]
    part_rows = shard_rows // parts
    over_dp = lambda value, bits: flip(value, "dp", parts, bits)
    over_z = lambda value, bits: flip(value, "fsdp", shards, bits * CORES)
    over_core = lambda value: flip(value, "fsdp", shards, 1)

    def over_split(value, dp_bits, z_bits):
        pairs = []
        for i in range(parts):
            for j in range(shards):
                core = j % CORES
                pairs.append((i * shards + j, (i ^ dp_bits[core]) * shards + (j ^ (z_bits[core] * CORES))))
        return lax.ppermute(value, ("dp", "fsdp"), pairs)

    near_both = (CORES * part_rows, key_width)

    def joined(*values):
        rows = len(values) * part_rows
        outs = [((rows, key_width), BF16)]
        return call(functools.partial(join_kernel, part_rows), outs, [(vmem, value) for value in values], "join")[0]

    matrix = frozen_key_matrix
    part = ((part_rows, key_width), BF16)
    near, far = call(start_kernel, [part, part], [(vmem, matrix)], "start")
    z1, z2 = over_z(near, 1), over_z(near, 2)
    (info,) = call(info_kernel, [((1, HD), F32)], [(vmem, adapter_offset)], "info")
    offsets = [info] + [over_dp(info, bits) for bits in range(1, parts)]
    held = call(
        hold_kernel,
        [((1, HD), F32), ((stored, rank, down_width), F32), (adapter_up_factor.shape, F32)],
        [(vmem, loss_row_count), (vmem, jnp.swapaxes(adapter_down_factor, 1, 2)), (vmem, adapter_up_factor)],
        "hold",
    )
    offsets, held = lax.optimization_barrier((offsets, held))
    wide = down_width + up_width + HD
    slots, own, sooner, later = call(
        messages_kernel,
        [((parts, HD), F32), ((rank, wide), F32), ((2 * rank, wide), F32), ((rank, wide), F32)],
        [(vmem, value) for value in (*offsets, *held)],
        "adapter_messages",
    )
    z1, z2 = ordered((z1, z2), sooner)
    sooner = over_split(sooner, (1, 2), (0, 0))
    z3 = over_z(z2, 1)
    z1_pair, z2_pair, sooner = lax.optimization_barrier((over_core(z1), over_core(z2), sooner))
    m12 = joined(z1, z1_pair, z2, z2_pair)
    xy12 = over_split(m12, (1, 2), (0, 0))
    d1 = over_z(ordered(far, m12), 1)
    (onward,) = call(pass_on_kernel, [((2 * rank, wide), F32)], [(vmem, later), (vmem, sooner)], "pass_on")
    later = over_split(onward, (2, 1), (0, 0))
    d3 = over_z(ordered(far, d1), 3)
    z3, matrix_pair = lax.optimization_barrier((z3, over_core(ordered(matrix, m12))))
    m3 = joined(z3, over_core(z3))
    xy3 = over_split(m3, (1, 2), (0, 0))
    xy12 = ordered(xy12, m3)
    (m4,) = call(functools.partial(take_kernel, part_rows, (2,)), [part], [(vmem, xy12)], "take")
    xy4 = over_split(m4, (2, 1), (0, 0))
    def piece(z, dp_bits, core, count=part_rows, first=0):
        pair = lambda value: value if isinstance(value, tuple) else (value, value)
        dp_bits = None if dp_bits is None else pair(dp_bits)
        return dict(z=pair(z), dp=dp_bits, core=core, rows=count, first=first)

    def two(z, dp_bits, core=0, first=0):
        return [piece(z, dp_bits, core, first=first), piece(z, dp_bits, 1 - core, first=first + part_rows)]

    def flat(batch):
        buffers = [value for value, _ in batch]
        pieces = [dict(item, buffer=index) for index, (_, items) in enumerate(batch) for item in items]
        return buffers, pieces

    def base(before, batch):
        buffers, pieces = flat(batch)
        (total,) = call(
            functools.partial(base_kernel, pieces, (part_rows, parts)),
            [((rows, key_width), F32)],
            [(vmem, tokens), (vmem, before)] + [(vmem, value) for value in buffers],
            "base",
        )
        return total

    split, up, low_rank, total, told = call(
        low_rank_kernel,
        [
            ((2 * rank, model_width), BF16),
            ((rank, key_width), F32),
            ((rows, rank), F32),
            ((rows, key_width), F32),
            ((parts, HD), F32),
        ],
        [(vmem, value) for value in (tokens, slots, own, sooner, later)],
        "low_rank",
    )
    batch0 = [
        (matrix, [piece(0, None, 0, shard_rows)]),
        (matrix_pair, [piece(0, None, 1, shard_rows)]),
        (m12, two(1, 0) + two(2, 0, 0, CORES * part_rows)),
        (xy12, two(1, (1, 2)) + two(2, (1, 2), 0, CORES * part_rows)),
        (m3, two(3, 0)),
    ]
    total = base(total, batch0)
    xy12, xy3, xy4, d1, d3, total = lax.optimization_barrier((xy12, xy3, xy4, d1, d3, total))
    batch1 = [
        (d1, [piece(1, 3, 0)]),
        (d3, [piece(3, 3, 0)]),
        (xy3, two(3, (1, 2))),
        (xy4, [piece(2, 3, 0)]),
    ]
    total = base(total, batch1)
    batch2 = [
        (over_core(xy12), two(1, (2, 1), 1) + two(2, (2, 1), 1, CORES * part_rows)),
        (over_core(d1), [piece(1, 3, 1)]),
        (over_core(d3), [piece(3, 3, 1)]),
        (over_core(xy3), two(3, (2, 1), 1)),
        (over_core(xy4), [piece(2, 3, 1)]),
    ]
    buffers, pieces = flat(batch2)
    keys, pre_low, low_grad, *grads = call(
        functools.partial(middle_kernel, pieces, (part_rows, parts)),
        [((rows, key_width), BF16), ((rows, key_width), BF16), ((rows, rank), F32)] + [((rank, down_width + up_width), F32)] * parts,
        [(vmem, value) for value in (told, tokens, total, cotangent, key_norm_gain.reshape(1, HD), low_rank, up)]
        + [(vmem, value) for value in buffers],
        "key_norm",
    )
    received = [grads[0]] + [over_dp(grads[bits], bits) for bits in range(1, parts)]
    buffers, pieces = flat(batch0 + batch1 + batch2)
    (input_grad,) = call(
        functools.partial(input_grad_kernel, pieces, (part_rows, parts)),
        [((rows, model_width), BF16)],
        [(vmem, pre_low), (vmem, low_grad), (vmem, split)] + [(vmem, value) for value in buffers],
        "input_grad",
    )
    down_sum, up_sum = call(
        sum_kernel,
        [((stored, rank, down_width), F32), ((stored, rank, up_width), F32)],
        [(vmem, told)] + [(vmem, value) for value in received],
        "grad_sum",
    )
    return keys, input_grad, jnp.swapaxes(down_sum, 1, 2), up_sum


def on_device_any(
    tokens,
    frozen_key_matrix,
    adapter_down_factor,
    adapter_up_factor,
    key_norm_gain,
    adapter_offset,
    loss_row_count,
    cotangent,
):
    row_count = tokens.shape[0]
    key_width = frozen_key_matrix.shape[1]
    stored_values = adapter_down_factor.shape[0]
    slot_value = adapter_offset[0, 0]
    live_count = loss_row_count[0, 0]
    selector = jnp.arange(stored_values, dtype=jnp.int32) == slot_value
    counted = jnp.where(selector, live_count, 0)
    summed_rows = lax.psum(counted, "dp")
    adapter_total = jnp.sum(jnp.where(selector, summed_rows, 0)).astype(F32)
    down_whole = lax.all_gather(adapter_down_factor, "dp", axis=1, tiled=True)
    up_whole = lax.all_gather(adapter_up_factor, "dp", axis=2, tiled=True)
    down_projection = lax.dynamic_index_in_dim(down_whole, slot_value, 0, keepdims=False)
    up_projection = lax.dynamic_index_in_dim(up_whole, slot_value, 0, keepdims=False)
    weight = lax.all_gather(frozen_key_matrix, "fsdp", axis=0, tiled=True)
    frozen_output = jnp.dot(tokens, weight, preferred_element_type=F32)
    tokens_float = tokens.astype(F32)
    lowrank_output = jnp.dot(tokens_float, down_projection, precision=HIGHEST)
    projected_keys = frozen_output + adapter_scale * jnp.dot(lowrank_output, up_projection, precision=HIGHEST)
    shaped = projected_keys.reshape(row_count, -1, HD)
    mean_square = jnp.mean(shaped * shaped, axis=-1, keepdims=True)
    inverse_rms = lax.rsqrt(mean_square + norm_eps)
    normed = shaped * inverse_rms
    keys = (normed * key_norm_gain).reshape(row_count, key_width).astype(BF16)
    row_mask = (jnp.arange(row_count, dtype=jnp.int32) < live_count).astype(F32)
    row_grad = cotangent.astype(F32) * row_mask[:, None] * (row_count / adapter_total)
    scaled_grad = row_grad.reshape(normed.shape) * key_norm_gain
    along_norm = jnp.mean(scaled_grad * normed, axis=-1, keepdims=True)
    prenorm_gradient = (inverse_rms * (scaled_grad - normed * along_norm)).reshape(row_count, key_width)
    pre_grad_low = prenorm_gradient.astype(BF16)
    lowrank_gradient = adapter_scale * jnp.dot(prenorm_gradient, up_projection.T, precision=HIGHEST)
    input_base = lax.dot_general(pre_grad_low, weight, (((1,), (1,)), ((), ())), preferred_element_type=F32)
    input_grad = (input_base + jnp.dot(lowrank_gradient, down_projection.T, precision=HIGHEST)).astype(BF16)
    down_grad = lax.dot_general(tokens_float, lowrank_gradient, (((0,), (0,)), ((), ())), precision=HIGHEST)
    up_factor_gradient = adapter_scale * lax.dot_general(
        lowrank_output, prenorm_gradient, (((0,), (0,)), ((), ())), precision=HIGHEST
    )
    selector_float = selector.astype(F32)
    down_terms = selector_float[:, None, None] * down_grad[None]
    up_terms = selector_float[:, None, None] * up_factor_gradient[None]
    down_sum = lax.psum_scatter(down_terms, "dp", scatter_dimension=1, tiled=True)
    up_sum = lax.psum_scatter(up_terms, "dp", scatter_dimension=2, tiled=True)
    return keys, input_grad, down_sum, up_sum


def solution(mesh):
    placed = (
        P(("dp", "fsdp"), None),
        P("fsdp", None),
        P("fsdp", "dp", None),
        P("fsdp", None, "dp"),
        P(),
        P("dp", "fsdp"),
        P("dp", "fsdp"),
        P(("dp", "fsdp"), None),
    )
    sizes = mesh.shape["dp"], mesh.shape["fsdp"]
    lines = sizes == (4, 4 * CORES)
    return jax.shard_map(
        functools.partial(on_device_lines, sizes) if lines else on_device_any,
        mesh=mesh,
        in_specs=placed,
        out_specs=(
            P(("dp", "fsdp"), None),
            P(("dp", "fsdp"), None),
            P("fsdp", "dp", None),
            P("fsdp", None, "dp"),
        ),
        check_vma=False,
    )
```

```python
import functools

import jax
import jax.numpy as jnp
from jax import lax
from jax.experimental import pallas as pl
from jax.experimental.pallas import tpu as pltpu
from jax.sharding import PartitionSpec as P

HD = 128
CORES = 2

adapter_scale = 2.0
norm_eps = 1e-06

F32 = jnp.float32
BF16 = jnp.bfloat16
HIGHEST = lax.Precision.HIGHEST
VMEM_LIMIT = 8 * 2**20

vmem = pl.BlockSpec(memory_space=pltpu.VMEM)
smem = pl.BlockSpec(memory_space=pltpu.SMEM)
hbm = pl.BlockSpec(memory_space=pltpu.HBM)


def split_two(value):
    high = value.astype(BF16)
    low = (value - high.astype(F32)).astype(BF16)
    return high, low


def call(kernel, outs, ins, name, moved=0):
    return pl.pallas_call(
        kernel,
        out_shape=[jax.ShapeDtypeStruct(shape, dtype) for shape, dtype in outs],
        in_specs=[spec for spec, _ in ins],
        out_specs=[vmem] * len(outs),
        compiler_params=pltpu.CompilerParams(vmem_limit_bytes=VMEM_LIMIT),
        cost_estimate=pl.CostEstimate(flops=0, bytes_accessed=moved, transcendentals=0),
        name=name,
    )(*[value for _, value in ins])


def position():
    fsdp = lax.axis_index("fsdp")
    return lax.axis_index("dp"), lax.div(fsdp, CORES), lax.rem(fsdp, CORES)


def part_kernel(bits, *refs):
    out = refs[-1]
    rows = out.shape[0] // (len(refs) - 1)
    part = lax.axis_index("dp") ^ bits
    for index, matrix in enumerate(refs[:-1]):
        out[index * rows : (index + 1) * rows] = matrix[pl.ds(pl.multiple_of(part * rows, rows), rows), :]


def info_kernel(offset, info):
    info[...] = jnp.broadcast_to(offset[...].astype(F32), info.shape)


def hold_kernel(count, down, up, count_held, down_held, up_held):
    count_held[...] = jnp.broadcast_to(count[...].astype(F32), count_held.shape)
    down_held[...] = down[...]
    up_held[...] = up[...]


def chosen(stored, slot):
    return sum(jnp.where(slot == index, stored[index], 0.0) for index in range(stored.shape[0]))


def messages_kernel(*refs):
    parts = len(refs) - 7
    offsets, (count, down, up), (slots, own, sooner, later) = refs[:parts], refs[parts : parts + 3], refs[parts + 3 :]
    rank, width = down.shape[1], down.shape[2]
    wide = width + up.shape[2]
    first_core = position()[2] == 0
    for partner, offset in enumerate(offsets):
        slots[partner : partner + 1, :] = offset[...]
    near, side, beside, far = (offset[:, :1] for offset in offsets)
    wanted = jnp.where(first_core, side, beside), jnp.where(first_core, beside, side)
    for slot, out, first in ((near, own, 0), (wanted[0], sooner, 0), (wanted[1], later, 0), (far, sooner, rank)):
        rows = pl.ds(first, rank)
        out[rows, :width] = chosen(down, slot)
        out[rows, width:wide] = chosen(up, slot)
        out[rows, wide:] = jnp.broadcast_to(count[...], (rank, HD))


def pass_on_kernel(later, received, out):
    rank = later.shape[0]
    out[:rank] = later[...]
    out[rank:] = received[rank:]


def take_kernel(each, wanted, value, out):
    for index, place in enumerate(wanted):
        out[index * each : (index + 1) * each] = value[place * each : (place + 1) * each]


def join_kernel(each, *refs):
    out, first = refs[-1], 0
    for ref in refs[:-1]:
        rows = each or ref.shape[0]
        out[first : first + rows] = ref[:rows]
        first += rows


def low_rank_kernel(tokens, slots, own, sooner, later, split, up, low_rank, total, told):
    rank = low_rank.shape[1]
    messages = own, sooner.at[:rank], later.at[:rank], later.at[rank:]
    parts = len(messages)
    down_width = tokens.shape[1] // parts
    up_width = up.shape[1] // parts
    dp, _, core = position()
    lane = lax.broadcasted_iota(jnp.int32, (1, HD), 1)
    counts = [message[:1, down_width + up_width :] for message in messages]
    counts[1:3] = jnp.where(core == 0, counts[1], counts[2]), jnp.where(core == 0, counts[2], counts[1])
    for partner, count in enumerate(counts):
        told[partner : partner + 1, :] = jnp.where(lane == 0, slots[partner : partner + 1, :], count)
    partners = 0, jnp.where(core == 0, 1, 2), jnp.where(core == 0, 2, 1), 3
    for partner, message in zip(partners, messages):
        part = dp ^ partner
        columns = pl.ds(pl.multiple_of(part * down_width, 128), down_width)
        high, low = split_two(message[:, :down_width])
        split[:rank, columns] = high
        split[rank:, columns] = low
        columns = pl.ds(pl.multiple_of(part * up_width, 128), up_width)
        up[:, columns] = message[:, down_width : down_width + up_width]
    both = lax.dot_general(tokens[...], split[...], (((1,), (1,)), ((), ())), preferred_element_type=F32)
    low_rank[...] = both[:, :rank] + both[:, rank:]
    total[...] = adapter_scale * jnp.dot(low_rank[...], up[...], precision=HIGHEST, preferred_element_type=F32)


def by_core(place, value):
    first, second = value
    return first if first == second else jnp.where(place[2] == 0, first, second)


def column_of(place, piece, part_rows, parts):
    shard = (place[1] ^ by_core(place, piece["z"])) * CORES + (place[2] ^ piece["core"])
    part = 0 if piece["dp"] is None else place[0] ^ by_core(place, piece["dp"])
    return pl.multiple_of((shard * parts + part) * part_rows, 128)


def base_sum(place, rows, total, buffers, pieces, sizes):
    for piece in pieces:
        columns = pl.ds(column_of(place, piece, *sizes), piece["rows"])
        part = pl.ds(piece["first"], piece["rows"])
        left = jnp.concatenate([ref[:, columns] for ref in rows], axis=0) if len(rows) > 1 else rows[0][:, columns]
        value = jnp.dot(left, buffers[piece["buffer"]][part, :], preferred_element_type=F32)
        total = value if total is None else total + value
    return total


def base_kernel(pieces, alone, sizes, tokens, tokens_pair, before, before_pair, *refs):
    place = position()
    buffers, (total, total_pair) = refs[:-2], refs[-2:]
    count = tokens.shape[0]
    both = base_sum(place, (tokens, tokens_pair), None, buffers, alone, sizes)
    total[...] = base_sum(place, (tokens,), before[...] + both[:count], buffers, pieces, sizes)
    total_pair[...] = before_pair[...] + both[count:]


def middle_kernel(parts, told, *refs):
    place = position()
    (tokens, own, received, cotangent, gain, low_rank, up), refs = refs[:7], refs[7:]
    (keys, pre_low, low_grad), grads = refs[:3], refs[3:]
    projected = own[...] + received[...]
    rows, width = projected.shape
    gains = gain[...]
    slots, counts = told[:, :1], told[:, 1:2]
    adapter_total = jnp.sum(jnp.where(slots == slots[:1], counts, 0.0), axis=0, keepdims=True)
    live = lax.broadcasted_iota(jnp.int32, (rows, 1), 0).astype(F32) < counts[:1]
    weight = rows / jnp.broadcast_to(adapter_total, (rows, 1))
    weight = jnp.where(live, weight, 0.0)
    heads = []
    for head in range(width // HD):
        columns = slice(head * HD, (head + 1) * HD)
        values = projected[:, columns]
        inverse = lax.rsqrt(jnp.mean(values * values, axis=-1, keepdims=True) + norm_eps)
        normed = values * inverse
        keys[:, columns] = (normed * gains).astype(BF16)
        scaled = cotangent[:, columns].astype(F32) * weight * gains
        along = jnp.mean(scaled * normed, axis=-1, keepdims=True)
        heads.append(inverse * (scaled - normed * along))
    pre = jnp.concatenate(heads, axis=-1)
    pre_low[...] = pre.astype(BF16)
    grad = adapter_scale * lax.dot_general(
        pre, up[...], (((1,), (1,)), ((), ())), precision=HIGHEST, preferred_element_type=F32
    )
    low_grad[...] = grad
    up_grad = adapter_scale * lax.dot_general(
        low_rank[...], pre, (((0,), (0,)), ((), ())), precision=HIGHEST, preferred_element_type=F32
    )
    rank = grad.shape[1]
    split = jnp.concatenate(split_two(grad), axis=-1)
    down_width, up_width = tokens.shape[1] // parts, width // parts
    for partner, out in enumerate(grads):
        part = place[0] ^ partner
        columns = pl.ds(pl.multiple_of(part * down_width, 128), down_width)
        both = lax.dot_general(split, tokens[:, columns], (((0,), (0,)), ((), ())), preferred_element_type=F32)
        out[:, :down_width] = (both[:rank] + both[rank:]).astype(out.dtype)
        for other in range(parts):

            @pl.when(part == other)
            def _():
                out[:, down_width:] = up_grad[:, other * up_width : (other + 1) * up_width].astype(out.dtype)


def input_grad_kernel(pieces, sizes, pre_low, low_grad, split, *refs):
    place = position()
    buffers, out = refs[:-1], refs[-1]
    rank = low_grad.shape[1]
    high, low = split_two(low_grad[...])
    left = jnp.concatenate([high, high, low], axis=-1)
    for piece in pieces:
        columns = pl.ds(column_of(place, piece, *sizes), piece["rows"])
        rows = pl.ds(piece["first"], piece["rows"])
        value = lax.dot_general(
            pre_low[...], buffers[piece["buffer"]][rows, :], (((1,), (1,)), ((), ())), preferred_element_type=F32
        )
        right = jnp.concatenate([split[:, columns], split[:rank, columns]], axis=0)
        value = value + jnp.dot(left, right, preferred_element_type=F32)
        out[:, columns] = value.astype(BF16)


def sum_kernel(told, *refs):
    grads, (down, up) = refs[:-2], refs[-2:]
    width = down.shape[2]
    for stored in range(down.shape[0]):
        total = jnp.zeros(grads[0].shape, F32)
        for partner, grad in enumerate(grads):
            slot = told[partner : partner + 1, :1]
            total = total + jnp.where(slot == stored, grad[...].astype(F32), 0.0)
        down[stored] = total[:, :width]
        up[stored] = total[:, width:]


def ordered(value, *earlier):
    return lax.optimization_barrier((value, *earlier))[0]


def flip(value, axis, size, bits):
    return lax.ppermute(value, axis, [(i, i ^ bits) for i in range(size)])


def on_device_lines(
    sizes,
    tokens,
    frozen_key_matrix,
    adapter_down_factor,
    adapter_up_factor,
    key_norm_gain,
    adapter_offset,
    loss_row_count,
    cotangent,
):
    parts, shards = sizes
    rows, model_width = tokens.shape
    key_width = frozen_key_matrix.shape[1]
    stored, down_width, rank = adapter_down_factor.shape
    up_width = adapter_up_factor.shape[2]
    shard_rows = frozen_key_matrix.shape[0]
    part_rows = shard_rows // parts
    over_dp = lambda value, bits: flip(value, "dp", parts, bits)
    over_z = lambda value, bits: flip(value, "fsdp", shards, bits * CORES)
    over_core = lambda value: flip(value, "fsdp", shards, 1)

    def over_split(value, dp_bits, z_bits):
        pairs = []
        for i in range(parts):
            for j in range(shards):
                core = j % CORES
                pairs.append((i * shards + j, (i ^ dp_bits[core]) * shards + (j ^ (z_bits[core] * CORES))))
        return lax.ppermute(value, ("dp", "fsdp"), pairs)

    near_both = (CORES * part_rows, key_width)

    def joined(*values):
        rows = len(values) * part_rows
        outs = [((rows, key_width), BF16)]
        return call(functools.partial(join_kernel, part_rows), outs, [(vmem, value) for value in values], "join")[0]

    matrix = frozen_key_matrix
    part = ((part_rows, key_width), BF16)
    (near,) = call(functools.partial(part_kernel, 0), [part], [(vmem, matrix)], "near")
    z2, z1 = over_z(near, 2), over_z(near, 1)
    (info,) = call(info_kernel, [((1, HD), F32)], [(vmem, adapter_offset)], "info")
    offsets = [info] + [over_dp(info, bits) for bits in range(1, parts)]
    held = call(
        hold_kernel,
        [((1, HD), F32), ((stored, rank, down_width), F32), (adapter_up_factor.shape, F32)],
        [(vmem, loss_row_count), (vmem, jnp.swapaxes(adapter_down_factor, 1, 2)), (vmem, adapter_up_factor)],
        "hold",
    )
    offsets, held = lax.optimization_barrier((offsets, held))
    wide = down_width + up_width + HD
    slots, own, sooner, later = call(
        messages_kernel,
        [((parts, HD), F32), ((rank, wide), F32), ((2 * rank, wide), F32), ((rank, wide), F32)],
        [(vmem, value) for value in (*offsets, *held)],
        "adapter_messages",
    )
    z2, z1 = ordered((z2, z1), sooner)
    sooner = over_split(sooner, (1, 2), (0, 0))
    z3 = over_z(z2, 1)
    z1_pair, z2_pair, sooner = lax.optimization_barrier((over_core(z1), over_core(z2), sooner))
    m12 = joined(z1, z1_pair, z2, z2_pair)
    xy12 = over_split(m12, (1, 2), (0, 0))
    matrix_pair, tokens_pair = over_core(ordered(matrix, m12)), over_core(ordered(tokens, m12))
    z3, matrix_pair, tokens_pair = lax.optimization_barrier((z3, matrix_pair, tokens_pair))
    (onward,) = call(pass_on_kernel, [((2 * rank, wide), F32)], [(vmem, later), (vmem, sooner)], "pass_on")
    later = over_split(onward, (2, 1), (0, 0))
    m3 = joined(z3, over_core(z3))
    xy3 = over_split(m3, (1, 2), (0, 0))
    (fars,) = call(
        functools.partial(part_kernel, parts - 1), [(near_both, BF16)], [(vmem, matrix), (vmem, matrix_pair)], "far"
    )
    d13 = over_split(ordered(fars, z3), (0, 0), (1, 3))
    xy12 = ordered(xy12, m3)
    (m4,) = call(functools.partial(take_kernel, part_rows, (2,)), [part], [(vmem, xy12)], "take")
    xy4 = over_split(m4, (2, 1), (0, 0))

    def piece(z, dp_bits, core, count=part_rows, first=0):
        pair = lambda value: value if isinstance(value, tuple) else (value, value)
        dp_bits = None if dp_bits is None else pair(dp_bits)
        return dict(z=pair(z), dp=dp_bits, core=core, rows=count, first=first)

    def two(z, dp_bits, core=0, first=0):
        return [piece(z, dp_bits, core, first=first), piece(z, dp_bits, 1 - core, first=first + part_rows)]

    def flat(batch):
        buffers = [value for value, _ in batch]
        pieces = [dict(item, buffer=index) for index, (_, items) in enumerate(batch) for item in items]
        return buffers, pieces

    def base(before, shared, alone):
        buffers, pieces = flat(shared + alone)
        mine = [item for item in pieces if item["buffer"] < len(shared)]
        lone = [item for item in pieces if item["buffer"] >= len(shared)]
        return call(
            functools.partial(base_kernel, mine, lone, (part_rows, parts)),
            [((rows, key_width), F32)] * 2,
            [(vmem, value) for value in (tokens, tokens_pair, *before, *buffers)],
            "base",
        )

    split, up, low_rank, total, told = call(
        low_rank_kernel,
        [
            ((2 * rank, model_width), BF16),
            ((rank, key_width), F32),
            ((rows, rank), F32),
            ((rows, key_width), F32),
            ((parts, HD), F32),
        ],
        [(vmem, value) for value in (tokens, slots, own, sooner, later)],
        "low_rank",
        moved=12 * 2**20,
    )
    last = CORES * part_rows
    shared = [
        (matrix, [piece(0, None, 0, shard_rows)]),
        (matrix_pair, [piece(0, None, 1, shard_rows)]),
        (m12, two(1, 0) + two(2, 0, 0, last)),
        (m3, two(3, 0)),
    ]
    early = [(xy12, two(1, (1, 2)) + two(2, (1, 2), 0, last))]
    totals = base((total, jnp.zeros_like(total)), shared, early)
    xy12, xy3, xy4, d13, totals = lax.optimization_barrier((xy12, xy3, xy4, d13, totals))
    late = [(xy3, two(3, (1, 2))), (d13, two((1, 3), 3)), (xy4, [piece(2, 3, 0)])]
    total, total_pair = base(totals, [], late)
    received = over_core(total_pair)
    lone = call(
        functools.partial(join_kernel, None),
        [((5 * part_rows, key_width), BF16)],
        [(vmem, value) for value in (xy3, d13, xy4)],
        "join",
    )[0]
    xy12_pair, lone_pair = over_core(ordered(xy12, received)), over_core(ordered(lone, received))
    keys, pre_low, low_grad, *grads = call(
        functools.partial(middle_kernel, parts),
        [((rows, key_width), BF16), ((rows, key_width), BF16), ((rows, rank), F32)]
        + [((rank, down_width + up_width), F32)] * parts,
        [
            (vmem, value)
            for value in (told, tokens, total, received, cotangent, key_norm_gain.reshape(1, HD), low_rank, up)
        ],
        "key_norm",
    )
    others = [
        (xy12_pair, two(1, (2, 1), 1) + two(2, (2, 1), 1, last)),
        (lone_pair, two(3, (2, 1), 1) + two((3, 1), 3, 1, last) + [piece(2, 3, 1, first=2 * last)]),
    ]
    received = [grads[0]] + [over_dp(grads[bits], bits) for bits in range(1, parts)]
    buffers, pieces = flat(shared + early + late + others)
    (input_grad,) = call(
        functools.partial(input_grad_kernel, pieces, (part_rows, parts)),
        [((rows, model_width), BF16)],
        [(vmem, pre_low), (vmem, low_grad), (vmem, split)] + [(vmem, value) for value in buffers],
        "input_grad",
    )
    received, input_grad = lax.optimization_barrier((received, input_grad))
    down_sum, up_sum = call(
        sum_kernel,
        [((stored, rank, down_width), F32), ((stored, rank, up_width), F32)],
        [(vmem, told)] + [(vmem, value) for value in received],
        "grad_sum",
    )
    return keys, input_grad, jnp.swapaxes(down_sum, 1, 2), up_sum


def on_device_any(
    tokens,
    frozen_key_matrix,
    adapter_down_factor,
    adapter_up_factor,
    key_norm_gain,
    adapter_offset,
    loss_row_count,
    cotangent,
):
    row_count = tokens.shape[0]
    key_width = frozen_key_matrix.shape[1]
    stored_values = adapter_down_factor.shape[0]
    slot_value = adapter_offset[0, 0]
    live_count = loss_row_count[0, 0]
    selector = jnp.arange(stored_values, dtype=jnp.int32) == slot_value
    counted = jnp.where(selector, live_count, 0)
    summed_rows = lax.psum(counted, "dp")
    adapter_total = jnp.sum(jnp.where(selector, summed_rows, 0)).astype(F32)
    down_whole = lax.all_gather(adapter_down_factor, "dp", axis=1, tiled=True)
    up_whole = lax.all_gather(adapter_up_factor, "dp", axis=2, tiled=True)
    down_projection = lax.dynamic_index_in_dim(down_whole, slot_value, 0, keepdims=False)
    up_projection = lax.dynamic_index_in_dim(up_whole, slot_value, 0, keepdims=False)
    weight = lax.all_gather(frozen_key_matrix, "fsdp", axis=0, tiled=True)
    frozen_output = jnp.dot(tokens, weight, preferred_element_type=F32)
    tokens_float = tokens.astype(F32)
    lowrank_output = jnp.dot(tokens_float, down_projection, precision=HIGHEST)
    projected_keys = frozen_output + adapter_scale * jnp.dot(lowrank_output, up_projection, precision=HIGHEST)
    shaped = projected_keys.reshape(row_count, -1, HD)
    mean_square = jnp.mean(shaped * shaped, axis=-1, keepdims=True)
    inverse_rms = lax.rsqrt(mean_square + norm_eps)
    normed = shaped * inverse_rms
    keys = (normed * key_norm_gain).reshape(row_count, key_width).astype(BF16)
    row_mask = (jnp.arange(row_count, dtype=jnp.int32) < live_count).astype(F32)
    row_grad = cotangent.astype(F32) * row_mask[:, None] * (row_count / adapter_total)
    scaled_grad = row_grad.reshape(normed.shape) * key_norm_gain
    along_norm = jnp.mean(scaled_grad * normed, axis=-1, keepdims=True)
    prenorm_gradient = (inverse_rms * (scaled_grad - normed * along_norm)).reshape(row_count, key_width)
    pre_grad_low = prenorm_gradient.astype(BF16)
    lowrank_gradient = adapter_scale * jnp.dot(prenorm_gradient, up_projection.T, precision=HIGHEST)
    input_base = lax.dot_general(pre_grad_low, weight, (((1,), (1,)), ((), ())), preferred_element_type=F32)
    input_grad = (input_base + jnp.dot(lowrank_gradient, down_projection.T, precision=HIGHEST)).astype(BF16)
    down_grad = lax.dot_general(tokens_float, lowrank_gradient, (((0,), (0,)), ((), ())), precision=HIGHEST)
    up_factor_gradient = adapter_scale * lax.dot_general(
        lowrank_output, prenorm_gradient, (((0,), (0,)), ((), ())), precision=HIGHEST
    )
    selector_float = selector.astype(F32)
    down_terms = selector_float[:, None, None] * down_grad[None]
    up_terms = selector_float[:, None, None] * up_factor_gradient[None]
    down_sum = lax.psum_scatter(down_terms, "dp", scatter_dimension=1, tiled=True)
    up_sum = lax.psum_scatter(up_terms, "dp", scatter_dimension=2, tiled=True)
    return keys, input_grad, down_sum, up_sum


def solution(mesh):
    placed = (
        P(("dp", "fsdp"), None),
        P("fsdp", None),
        P("fsdp", "dp", None),
        P("fsdp", None, "dp"),
        P(),
        P("dp", "fsdp"),
        P("dp", "fsdp"),
        P(("dp", "fsdp"), None),
    )
    sizes = mesh.shape["dp"], mesh.shape["fsdp"]
    lines = sizes == (4, 4 * CORES)
    return jax.shard_map(
        functools.partial(on_device_lines, sizes) if lines else on_device_any,
        mesh=mesh,
        in_specs=placed,
        out_specs=(
            P(("dp", "fsdp"), None),
            P(("dp", "fsdp"), None),
            P("fsdp", "dp", None),
            P("fsdp", None, "dp"),
        ),
        check_vma=False,
    )
```

```python
import functools

import jax
import jax.numpy as jnp
from jax import lax
from jax.experimental import pallas as pl
from jax.experimental.pallas import tpu as pltpu
from jax.sharding import PartitionSpec as P

HD = 128
CORES = 2

adapter_scale = 2.0
norm_eps = 1e-06

F32 = jnp.float32
BF16 = jnp.bfloat16
HIGHEST = lax.Precision.HIGHEST
VMEM_LIMIT = 8 * 2**20

vmem = pl.BlockSpec(memory_space=pltpu.VMEM)
smem = pl.BlockSpec(memory_space=pltpu.SMEM)
hbm = pl.BlockSpec(memory_space=pltpu.HBM)


def split_two(value):
    high = value.astype(BF16)
    low = (value - high.astype(F32)).astype(BF16)
    return high, low


def call(kernel, outs, ins, name, moved=0, out=vmem, scratch=()):
    return pl.pallas_call(
        kernel,
        out_shape=[jax.ShapeDtypeStruct(shape, dtype) for shape, dtype in outs],
        in_specs=[spec for spec, _ in ins],
        out_specs=[out] * len(outs),
        scratch_shapes=scratch,
        compiler_params=pltpu.CompilerParams(vmem_limit_bytes=VMEM_LIMIT),
        cost_estimate=pl.CostEstimate(flops=0, bytes_accessed=moved, transcendentals=0),
        name=name,
    )(*[value for _, value in ins])


def position():
    fsdp = lax.axis_index("fsdp")
    return lax.axis_index("dp"), lax.div(fsdp, CORES), lax.rem(fsdp, CORES)


def part_kernel(bits, *refs):
    out = refs[-1]
    rows = out.shape[0] // (len(refs) - 1)
    part = lax.axis_index("dp") ^ bits
    for index, matrix in enumerate(refs[:-1]):
        out[index * rows : (index + 1) * rows] = matrix[pl.ds(pl.multiple_of(part * rows, rows), rows), :]


def info_kernel(offset, info):
    info[...] = jnp.broadcast_to(offset[...].astype(F32), info.shape)


def hold_kernel(count, down, up, count_held, down_held, up_held):
    count_held[...] = jnp.broadcast_to(count[...].astype(F32), count_held.shape)
    down_held[...] = down[...]
    up_held[...] = up[...]


def chosen(stored, slot):
    return sum(jnp.where(slot == index, stored[index], 0.0) for index in range(stored.shape[0]))


def messages_kernel(*refs):
    parts = len(refs) - 7
    offsets, (count, down, up), (slots, own, sooner, later) = refs[:parts], refs[parts : parts + 3], refs[parts + 3 :]
    rank, width = down.shape[1], down.shape[2]
    wide = width + up.shape[2]
    first_core = position()[2] == 0
    for partner, offset in enumerate(offsets):
        slots[partner : partner + 1, :] = offset[...]
    near, side, beside, far = (offset[:, :1] for offset in offsets)
    wanted = jnp.where(first_core, side, beside), jnp.where(first_core, beside, side)
    for slot, out, first in ((near, own, 0), (wanted[0], sooner, 0), (wanted[1], later, 0), (far, sooner, rank)):
        rows = pl.ds(first, rank)
        out[rows, :width] = chosen(down, slot)
        out[rows, width:wide] = chosen(up, slot)
        out[rows, wide:] = jnp.broadcast_to(count[...], (rank, HD))


def pass_on_kernel(later, received, out):
    rank = later.shape[0]
    out[:rank] = later[...]
    out[rank:] = received[rank:]


def take_kernel(each, wanted, value, out):
    for index, place in enumerate(wanted):
        out[index * each : (index + 1) * each] = value[place * each : (place + 1) * each]


def join_kernel(each, *refs):
    out, first = refs[-1], 0
    for ref in refs[:-1]:
        rows = each or ref.shape[0]
        out[first : first + rows] = ref[:rows]
        first += rows


def low_rank_kernel(tokens, slots, own, sooner, later, split, up, low_rank, total, told):
    rank = low_rank.shape[1]
    messages = own, sooner.at[:rank], later.at[:rank], later.at[rank:]
    parts = len(messages)
    down_width = tokens.shape[1] // parts
    up_width = up.shape[1] // parts
    dp, _, core = position()
    lane = lax.broadcasted_iota(jnp.int32, (1, HD), 1)
    counts = [message[:1, down_width + up_width :] for message in messages]
    counts[1:3] = jnp.where(core == 0, counts[1], counts[2]), jnp.where(core == 0, counts[2], counts[1])
    for partner, count in enumerate(counts):
        told[partner : partner + 1, :] = jnp.where(lane == 0, slots[partner : partner + 1, :], count)
    partners = 0, jnp.where(core == 0, 1, 2), jnp.where(core == 0, 2, 1), 3
    for partner, message in zip(partners, messages):
        part = dp ^ partner
        columns = pl.ds(pl.multiple_of(part * down_width, 128), down_width)
        high, low = split_two(message[:, :down_width])
        split[:rank, columns] = high
        split[rank:, columns] = low
        columns = pl.ds(pl.multiple_of(part * up_width, 128), up_width)
        up[:, columns] = message[:, down_width : down_width + up_width]
    both = lax.dot_general(tokens[...], split[...], (((1,), (1,)), ((), ())), preferred_element_type=F32)
    low_rank[...] = both[:, :rank] + both[:, rank:]
    total[...] = adapter_scale * jnp.dot(low_rank[...], up[...], precision=HIGHEST, preferred_element_type=F32)


def by_core(place, value):
    first, second = value
    return first if first == second else jnp.where(place[2] == 0, first, second)


def column_of(place, piece, part_rows, parts):
    shard = (place[1] ^ by_core(place, piece["z"])) * CORES + (place[2] ^ piece["core"])
    part = 0 if piece["dp"] is None else place[0] ^ by_core(place, piece["dp"])
    return pl.multiple_of((shard * parts + part) * part_rows, 128)


def base_sum(place, rows, total, buffers, pieces, sizes):
    for piece in pieces:
        columns = pl.ds(column_of(place, piece, *sizes), piece["rows"])
        part = pl.ds(piece["first"], piece["rows"])
        left = jnp.concatenate([ref[:, columns] for ref in rows], axis=0) if len(rows) > 1 else rows[0][:, columns]
        value = jnp.dot(left, buffers[piece["buffer"]][part, :], preferred_element_type=F32)
        total = value if total is None else total + value
    return total


def base_kernel(pieces, alone, sizes, tokens, tokens_pair, before, before_pair, *refs):
    place = position()
    buffers, (total, total_pair) = refs[:-2], refs[-2:]
    count = tokens.shape[0]
    both = base_sum(place, (tokens, tokens_pair), None, buffers, alone, sizes)
    total[...] = base_sum(place, (tokens,), before[...] + both[:count], buffers, pieces, sizes)
    total_pair[...] = before_pair[...] + both[count:]


def middle_kernel(parts, told, *refs):
    place = position()
    (tokens, own, received, cotangent, gain, low_rank, up), refs = refs[:7], refs[7:]
    (keys, pre_low, low_grad), grads = refs[:3], refs[3:]
    projected = own[...] + received[...]
    rows, width = projected.shape
    gains = gain[...]
    slots, counts = told[:, :1], told[:, 1:2]
    adapter_total = jnp.sum(jnp.where(slots == slots[:1], counts, 0.0), axis=0, keepdims=True)
    live = lax.broadcasted_iota(jnp.int32, (rows, 1), 0).astype(F32) < counts[:1]
    weight = rows / jnp.broadcast_to(adapter_total, (rows, 1))
    weight = jnp.where(live, weight, 0.0)
    heads = []
    for head in range(width // HD):
        columns = slice(head * HD, (head + 1) * HD)
        values = projected[:, columns]
        inverse = lax.rsqrt(jnp.mean(values * values, axis=-1, keepdims=True) + norm_eps)
        normed = values * inverse
        keys[:, columns] = (normed * gains).astype(BF16)
        scaled = cotangent[:, columns].astype(F32) * weight * gains
        along = jnp.mean(scaled * normed, axis=-1, keepdims=True)
        heads.append(inverse * (scaled - normed * along))
    pre = jnp.concatenate(heads, axis=-1)
    pre_low[...] = pre.astype(BF16)
    (pre_high, pre_rest), (up_high, up_rest), (low_high, low_rest) = map(split_two, (pre, up[...], low_rank[...]))
    rank = up.shape[0]
    both = lax.dot_general(
        jnp.concatenate([pre_high, pre_rest], axis=0),
        jnp.concatenate([up_high, up_rest], axis=0),
        (((1,), (1,)), ((), ())),
        preferred_element_type=F32,
    )
    grad = adapter_scale * (both[:rows, :rank] + both[:rows, rank:] + both[rows:, :rank])
    low_grad[...] = grad
    across = (((0,), (0,)), ((), ()))
    both = lax.dot_general(
        jnp.concatenate([low_high, low_rest], axis=-1), pre_high, across, preferred_element_type=F32
    )
    rest = lax.dot_general(low_high, pre_rest, across, preferred_element_type=F32)
    up_grad = adapter_scale * (both[:rank] + both[rank:] + rest)
    split = jnp.concatenate(split_two(grad), axis=-1)
    down_width, up_width = tokens.shape[1] // parts, width // parts
    for partner, out in enumerate(grads):
        part = place[0] ^ partner
        columns = pl.ds(pl.multiple_of(part * down_width, 128), down_width)
        both = lax.dot_general(split, tokens[:, columns], (((0,), (0,)), ((), ())), preferred_element_type=F32)
        out[:, :down_width] = (both[:rank] + both[rank:]).astype(out.dtype)
        for other in range(parts):

            @pl.when(part == other)
            def _():
                out[:, down_width:] = up_grad[:, other * up_width : (other + 1) * up_width].astype(out.dtype)


def input_grad_kernel(pieces, sizes, pre_low, low_grad, split, *refs):
    place = position()
    buffers, (out, held, copied) = refs[:-3], refs[-3:]
    rank = low_grad.shape[1]
    high, low = split_two(low_grad[...])
    left = jnp.concatenate([high, high, low], axis=-1)
    turned = pre_low[...].T
    copies = []
    for index, piece in enumerate(pieces):
        columns = pl.ds(column_of(place, piece, *sizes), piece["rows"])
        rows = pl.ds(piece["first"], piece["rows"])
        value = jnp.dot(buffers[piece["buffer"]][rows, :], turned, preferred_element_type=F32).T
        right = jnp.concatenate([split[:, columns], split[:rank, columns]], axis=0)
        value = value + jnp.dot(left, right, preferred_element_type=F32)
        held[:, columns] = value.astype(BF16)
        copies.append(pltpu.make_async_copy(held.at[:, columns], out.at[:, columns], copied.at[index]))
        copies[-1].start()
    for copy in copies:
        copy.wait()


def sum_kernel(told, *refs):
    grads, (down, up) = refs[:-2], refs[-2:]
    width = down.shape[2]
    for stored in range(down.shape[0]):
        total = jnp.zeros(grads[0].shape, F32)
        for partner, grad in enumerate(grads):
            slot = told[partner : partner + 1, :1]
            total = total + jnp.where(slot == stored, grad[...].astype(F32), 0.0)
        down[stored] = total[:, :width]
        up[stored] = total[:, width:]


def ordered(value, *earlier):
    return lax.optimization_barrier((value, *earlier))[0]


def flip(value, axis, size, bits):
    return lax.ppermute(value, axis, [(i, i ^ bits) for i in range(size)])


def on_device_lines(
    sizes,
    tokens,
    frozen_key_matrix,
    adapter_down_factor,
    adapter_up_factor,
    key_norm_gain,
    adapter_offset,
    loss_row_count,
    cotangent,
):
    parts, shards = sizes
    rows, model_width = tokens.shape
    key_width = frozen_key_matrix.shape[1]
    stored, down_width, rank = adapter_down_factor.shape
    up_width = adapter_up_factor.shape[2]
    shard_rows = frozen_key_matrix.shape[0]
    part_rows = shard_rows // parts
    over_dp = lambda value, bits: flip(value, "dp", parts, bits)
    over_z = lambda value, bits: flip(value, "fsdp", shards, bits * CORES)
    over_core = lambda value: flip(value, "fsdp", shards, 1)

    def over_split(value, dp_bits, z_bits):
        pairs = []
        for i in range(parts):
            for j in range(shards):
                core = j % CORES
                pairs.append((i * shards + j, (i ^ dp_bits[core]) * shards + (j ^ (z_bits[core] * CORES))))
        return lax.ppermute(value, ("dp", "fsdp"), pairs)

    near_both = (CORES * part_rows, key_width)

    def joined(*values):
        rows = len(values) * part_rows
        outs = [((rows, key_width), BF16)]
        return call(functools.partial(join_kernel, part_rows), outs, [(vmem, value) for value in values], "join")[0]

    matrix = frozen_key_matrix
    part = ((part_rows, key_width), BF16)
    (near,) = call(functools.partial(part_kernel, 0), [part], [(vmem, matrix)], "near")
    z2, z1 = over_z(near, 2), over_z(near, 1)
    (info,) = call(info_kernel, [((1, HD), F32)], [(vmem, adapter_offset)], "info")
    offsets = [info] + [over_dp(info, bits) for bits in range(1, parts)]
    held = call(
        hold_kernel,
        [((1, HD), F32), ((stored, rank, down_width), F32), (adapter_up_factor.shape, F32)],
        [(vmem, loss_row_count), (vmem, jnp.swapaxes(adapter_down_factor, 1, 2)), (vmem, adapter_up_factor)],
        "hold",
    )
    offsets, held = lax.optimization_barrier((offsets, held))
    wide = down_width + up_width + HD
    slots, own, sooner, later = call(
        messages_kernel,
        [((parts, HD), F32), ((rank, wide), F32), ((2 * rank, wide), F32), ((rank, wide), F32)],
        [(vmem, value) for value in (*offsets, *held)],
        "adapter_messages",
    )
    z2, z1 = ordered((z2, z1), sooner)
    sooner = over_split(sooner, (1, 2), (0, 0))
    z3 = over_z(z2, 1)
    z1_pair, z2_pair, sooner = lax.optimization_barrier((over_core(z1), over_core(z2), sooner))
    m12 = joined(z1, z1_pair, z2, z2_pair)
    xy12 = over_split(m12, (1, 2), (0, 0))
    matrix_pair, tokens_pair = over_core(ordered(matrix, m12)), over_core(ordered(tokens, m12))
    z3, matrix_pair, tokens_pair = lax.optimization_barrier((z3, matrix_pair, tokens_pair))
    (onward,) = call(pass_on_kernel, [((2 * rank, wide), F32)], [(vmem, later), (vmem, sooner)], "pass_on")
    later = over_split(onward, (2, 1), (0, 0))
    m3 = joined(z3, over_core(z3))
    xy3 = over_split(m3, (1, 2), (0, 0))
    (fars,) = call(
        functools.partial(part_kernel, parts - 1), [(near_both, BF16)], [(vmem, matrix), (vmem, matrix_pair)], "far"
    )
    d13 = over_split(ordered(fars, z3), (0, 0), (1, 3))
    xy12 = ordered(xy12, m3)
    (m4,) = call(functools.partial(take_kernel, part_rows, (2,)), [part], [(vmem, xy12)], "take")
    xy4 = over_split(m4, (2, 1), (0, 0))

    def piece(z, dp_bits, core, count=part_rows, first=0):
        pair = lambda value: value if isinstance(value, tuple) else (value, value)
        dp_bits = None if dp_bits is None else pair(dp_bits)
        return dict(z=pair(z), dp=dp_bits, core=core, rows=count, first=first)

    def two(z, dp_bits, core=0, first=0):
        return [piece(z, dp_bits, core, first=first), piece(z, dp_bits, 1 - core, first=first + part_rows)]

    def flat(batch):
        buffers = [value for value, _ in batch]
        pieces = [dict(item, buffer=index) for index, (_, items) in enumerate(batch) for item in items]
        return buffers, pieces

    def base(before, shared, alone):
        buffers, pieces = flat(shared + alone)
        mine = [item for item in pieces if item["buffer"] < len(shared)]
        lone = [item for item in pieces if item["buffer"] >= len(shared)]
        return call(
            functools.partial(base_kernel, mine, lone, (part_rows, parts)),
            [((rows, key_width), F32)] * 2,
            [(vmem, value) for value in (tokens, tokens_pair, *before, *buffers)],
            "base",
        )

    split, up, low_rank, total, told = call(
        low_rank_kernel,
        [
            ((2 * rank, model_width), BF16),
            ((rank, key_width), F32),
            ((rows, rank), F32),
            ((rows, key_width), F32),
            ((parts, HD), F32),
        ],
        [(vmem, value) for value in (tokens, slots, own, sooner, later)],
        "low_rank",
        moved=12 * 2**20,
    )
    last = CORES * part_rows
    shared = [
        (matrix, [piece(0, None, 0, shard_rows)]),
        (matrix_pair, [piece(0, None, 1, shard_rows)]),
        (m12, two(1, 0) + two(2, 0, 0, last)),
        (m3, two(3, 0)),
    ]
    early = [(xy12, two(1, (1, 2)) + two(2, (1, 2), 0, last))]
    totals = base((total, jnp.zeros_like(total)), shared, early)
    xy12, xy3, xy4, d13, totals = lax.optimization_barrier((xy12, xy3, xy4, d13, totals))
    late = [(xy3, two(3, (1, 2))), (d13, two((1, 3), 3)), (xy4, [piece(2, 3, 0)])]
    total, total_pair = base(totals, [], late)
    received = over_core(total_pair)
    lone = call(
        functools.partial(join_kernel, None),
        [((5 * part_rows, key_width), BF16)],
        [(vmem, value) for value in (xy3, d13, xy4)],
        "join",
    )[0]
    xy12_pair, lone_pair = over_core(ordered(xy12, received)), over_core(ordered(lone, received))
    keys, pre_low, low_grad, *grads = call(
        functools.partial(middle_kernel, parts),
        [((rows, key_width), BF16), ((rows, key_width), BF16), ((rows, rank), F32)]
        + [((rank, down_width + up_width), F32)]
        + [((rank, down_width + up_width), BF16)] * (parts - 1),
        [
            (vmem, value)
            for value in (told, tokens, total, received, cotangent, key_norm_gain.reshape(1, HD), low_rank, up)
        ],
        "key_norm",
    )
    others = [
        (xy12_pair, two(1, (2, 1), 1) + two(2, (2, 1), 1, last)),
        (lone_pair, two(3, (2, 1), 1) + two((3, 1), 3, 1, last) + [piece(2, 3, 1, first=2 * last)]),
    ]
    received = [grads[0]] + [over_dp(grads[bits], bits) for bits in range(1, parts)]
    buffers, pieces = flat(shared + early + late + others)
    (input_grad,) = call(
        functools.partial(input_grad_kernel, pieces, (part_rows, parts)),
        [((rows, model_width), BF16)],
        [(vmem, pre_low), (vmem, low_grad), (vmem, split)] + [(vmem, value) for value in buffers],
        "input_grad",
        out=hbm,
        scratch=[pltpu.VMEM((rows, model_width), BF16), pltpu.SemaphoreType.DMA((len(pieces),))],
    )
    received, input_grad = lax.optimization_barrier((received, input_grad))
    down_sum, up_sum = call(
        sum_kernel,
        [((stored, rank, down_width), F32), ((stored, rank, up_width), F32)],
        [(vmem, told)] + [(vmem, value) for value in received],
        "grad_sum",
    )
    return keys, input_grad, jnp.swapaxes(down_sum, 1, 2), up_sum


def on_device_any(
    tokens,
    frozen_key_matrix,
    adapter_down_factor,
    adapter_up_factor,
    key_norm_gain,
    adapter_offset,
    loss_row_count,
    cotangent,
):
    row_count = tokens.shape[0]
    key_width = frozen_key_matrix.shape[1]
    stored_values = adapter_down_factor.shape[0]
    slot_value = adapter_offset[0, 0]
    live_count = loss_row_count[0, 0]
    selector = jnp.arange(stored_values, dtype=jnp.int32) == slot_value
    counted = jnp.where(selector, live_count, 0)
    summed_rows = lax.psum(counted, "dp")
    adapter_total = jnp.sum(jnp.where(selector, summed_rows, 0)).astype(F32)
    down_whole = lax.all_gather(adapter_down_factor, "dp", axis=1, tiled=True)
    up_whole = lax.all_gather(adapter_up_factor, "dp", axis=2, tiled=True)
    down_projection = lax.dynamic_index_in_dim(down_whole, slot_value, 0, keepdims=False)
    up_projection = lax.dynamic_index_in_dim(up_whole, slot_value, 0, keepdims=False)
    weight = lax.all_gather(frozen_key_matrix, "fsdp", axis=0, tiled=True)
    frozen_output = jnp.dot(tokens, weight, preferred_element_type=F32)
    tokens_float = tokens.astype(F32)
    lowrank_output = jnp.dot(tokens_float, down_projection, precision=HIGHEST)
    projected_keys = frozen_output + adapter_scale * jnp.dot(lowrank_output, up_projection, precision=HIGHEST)
    shaped = projected_keys.reshape(row_count, -1, HD)
    mean_square = jnp.mean(shaped * shaped, axis=-1, keepdims=True)
    inverse_rms = lax.rsqrt(mean_square + norm_eps)
    normed = shaped * inverse_rms
    keys = (normed * key_norm_gain).reshape(row_count, key_width).astype(BF16)
    row_mask = (jnp.arange(row_count, dtype=jnp.int32) < live_count).astype(F32)
    row_grad = cotangent.astype(F32) * row_mask[:, None] * (row_count / adapter_total)
    scaled_grad = row_grad.reshape(normed.shape) * key_norm_gain
    along_norm = jnp.mean(scaled_grad * normed, axis=-1, keepdims=True)
    prenorm_gradient = (inverse_rms * (scaled_grad - normed * along_norm)).reshape(row_count, key_width)
    pre_grad_low = prenorm_gradient.astype(BF16)
    lowrank_gradient = adapter_scale * jnp.dot(prenorm_gradient, up_projection.T, precision=HIGHEST)
    input_base = lax.dot_general(pre_grad_low, weight, (((1,), (1,)), ((), ())), preferred_element_type=F32)
    input_grad = (input_base + jnp.dot(lowrank_gradient, down_projection.T, precision=HIGHEST)).astype(BF16)
    down_grad = lax.dot_general(tokens_float, lowrank_gradient, (((0,), (0,)), ((), ())), precision=HIGHEST)
    up_factor_gradient = adapter_scale * lax.dot_general(
        lowrank_output, prenorm_gradient, (((0,), (0,)), ((), ())), precision=HIGHEST
    )
    selector_float = selector.astype(F32)
    down_terms = selector_float[:, None, None] * down_grad[None]
    up_terms = selector_float[:, None, None] * up_factor_gradient[None]
    down_sum = lax.psum_scatter(down_terms, "dp", scatter_dimension=1, tiled=True)
    up_sum = lax.psum_scatter(up_terms, "dp", scatter_dimension=2, tiled=True)
    return keys, input_grad, down_sum, up_sum


def solution(mesh):
    placed = (
        P(("dp", "fsdp"), None),
        P("fsdp", None),
        P("fsdp", "dp", None),
        P("fsdp", None, "dp"),
        P(),
        P("dp", "fsdp"),
        P("dp", "fsdp"),
        P(("dp", "fsdp"), None),
    )
    sizes = mesh.shape["dp"], mesh.shape["fsdp"]
    lines = sizes == (4, 4 * CORES)
    return jax.shard_map(
        functools.partial(on_device_lines, sizes) if lines else on_device_any,
        mesh=mesh,
        in_specs=placed,
        out_specs=(
            P(("dp", "fsdp"), None),
            P(("dp", "fsdp"), None),
            P("fsdp", "dp", None),
            P("fsdp", None, "dp"),
        ),
        check_vma=False,
    )
```

```python
import functools

import jax
import jax.numpy as jnp
from jax import lax
from jax.experimental import pallas as pl
from jax.experimental.pallas import tpu as pltpu
from jax.sharding import PartitionSpec as P

HD = 128
CORES = 2

adapter_scale = 2.0
norm_eps = 1e-06

F32 = jnp.float32
BF16 = jnp.bfloat16
HIGHEST = lax.Precision.HIGHEST
VMEM_LIMIT = 8 * 2**20

vmem = pl.BlockSpec(memory_space=pltpu.VMEM)
smem = pl.BlockSpec(memory_space=pltpu.SMEM)
hbm = pl.BlockSpec(memory_space=pltpu.HBM)


def split_two(value):
    high = value.astype(BF16)
    low = (value - high.astype(F32)).astype(BF16)
    return high, low


def call(kernel, outs, ins, name, moved=0, out=vmem, scratch=()):
    return pl.pallas_call(
        kernel,
        out_shape=[jax.ShapeDtypeStruct(shape, dtype) for shape, dtype in outs],
        in_specs=[spec for spec, _ in ins],
        out_specs=out if isinstance(out, list) else [out] * len(outs),
        scratch_shapes=scratch,
        compiler_params=pltpu.CompilerParams(vmem_limit_bytes=VMEM_LIMIT),
        cost_estimate=pl.CostEstimate(flops=0, bytes_accessed=moved, transcendentals=0),
        name=name,
    )(*[value for _, value in ins])


def position():
    fsdp = lax.axis_index("fsdp")
    return lax.axis_index("dp"), lax.div(fsdp, CORES), lax.rem(fsdp, CORES)


def part_kernel(bits, *refs):
    out = refs[-1]
    rows = out.shape[0] // (len(refs) - 1)
    part = lax.axis_index("dp") ^ bits
    for index, matrix in enumerate(refs[:-1]):
        out[index * rows : (index + 1) * rows] = matrix[pl.ds(pl.multiple_of(part * rows, rows), rows), :]


def info_kernel(offset, info):
    info[...] = jnp.broadcast_to(offset[...].astype(F32), info.shape)


def hold_kernel(count, down, up, count_held, down_held, up_held):
    count_held[...] = jnp.broadcast_to(count[...].astype(F32), count_held.shape)
    down_held[...] = down[...]
    up_held[...] = up[...]


def chosen(stored, slot):
    return sum(jnp.where(slot == index, stored[index], 0.0) for index in range(stored.shape[0]))


def messages_kernel(*refs):
    parts = len(refs) - 7
    offsets, (count, down, up), (slots, own, sooner, later) = refs[:parts], refs[parts : parts + 3], refs[parts + 3 :]
    rank, width = down.shape[1], down.shape[2]
    wide = width + up.shape[2]
    first_core = position()[2] == 0
    for partner, offset in enumerate(offsets):
        slots[partner : partner + 1, :] = offset[...]
    near, side, beside, far = (offset[:, :1] for offset in offsets)
    wanted = jnp.where(first_core, side, beside), jnp.where(first_core, beside, side)
    for slot, out, first in ((near, own, 0), (wanted[0], sooner, 0), (wanted[1], later, 0), (far, sooner, rank)):
        rows = pl.ds(first, rank)
        out[rows, :width] = chosen(down, slot)
        out[rows, width:wide] = chosen(up, slot)
        out[rows, wide:] = jnp.broadcast_to(count[...], (rank, HD))


def pass_on_kernel(later, received, out):
    rank = later.shape[0]
    out[:rank] = later[...]
    out[rank:] = received[rank:]


def take_kernel(each, wanted, value, out):
    for index, place in enumerate(wanted):
        out[index * each : (index + 1) * each] = value[place * each : (place + 1) * each]


def join_kernel(each, *refs):
    out, first = refs[-1], 0
    for ref in refs[:-1]:
        rows = each or ref.shape[0]
        out[first : first + rows] = ref[:rows]
        first += rows


def low_rank_kernel(tokens, slots, own, sooner, later, split, up, low_rank, total, told):
    rank = low_rank.shape[1]
    messages = own, sooner.at[:rank], later.at[:rank], later.at[rank:]
    parts = len(messages)
    down_width = tokens.shape[1] // parts
    up_width = up.shape[1] // parts
    dp, _, core = position()
    lane = lax.broadcasted_iota(jnp.int32, (1, HD), 1)
    counts = [message[:1, down_width + up_width :] for message in messages]
    counts[1:3] = jnp.where(core == 0, counts[1], counts[2]), jnp.where(core == 0, counts[2], counts[1])
    for partner, count in enumerate(counts):
        told[partner : partner + 1, :] = jnp.where(lane == 0, slots[partner : partner + 1, :], count)
    partners = 0, jnp.where(core == 0, 1, 2), jnp.where(core == 0, 2, 1), 3
    for partner, message in zip(partners, messages):
        part = dp ^ partner
        columns = pl.ds(pl.multiple_of(part * down_width, 128), down_width)
        high, low = split_two(message[:, :down_width])
        split[:rank, columns] = high
        split[rank:, columns] = low
        columns = pl.ds(pl.multiple_of(part * up_width, 128), up_width)
        up[:, columns] = message[:, down_width : down_width + up_width]
    both = lax.dot_general(tokens[...], split[...], (((1,), (1,)), ((), ())), preferred_element_type=F32)
    low_rank[...] = both[:, :rank] + both[:, rank:]
    total[...] = adapter_scale * jnp.dot(low_rank[...], up[...], precision=HIGHEST, preferred_element_type=F32)


def by_core(place, value):
    first, second = value
    return first if first == second else jnp.where(place[2] == 0, first, second)


def column_of(place, piece, part_rows, parts):
    shard = (place[1] ^ by_core(place, piece["z"])) * CORES + (place[2] ^ piece["core"])
    part = 0 if piece["dp"] is None else place[0] ^ by_core(place, piece["dp"])
    return pl.multiple_of((shard * parts + part) * part_rows, 128)


def base_sum(place, rows, total, buffers, pieces, sizes):
    for piece in pieces:
        columns = pl.ds(column_of(place, piece, *sizes), piece["rows"])
        part = pl.ds(piece["first"], piece["rows"])
        left = jnp.concatenate([ref[:, columns] for ref in rows], axis=0) if len(rows) > 1 else rows[0][:, columns]
        value = jnp.dot(left, buffers[piece["buffer"]][part, :], preferred_element_type=F32)
        total = value if total is None else total + value
    return total


def base_kernel(pieces, alone, sizes, tokens, tokens_pair, before, before_pair, *refs):
    place = position()
    buffers, (total, total_pair) = refs[:-2], refs[-2:]
    count = tokens.shape[0]
    both = base_sum(place, (tokens, tokens_pair), None, buffers, alone, sizes)
    total[...] = base_sum(place, (tokens,), before[...] + both[:count], buffers, pieces, sizes)
    total_pair[...] = before_pair[...] + both[count:]


def middle_kernel(parts, told, *refs):
    place = position()
    (tokens, own, received, cotangent, gain, low_rank, up), refs = refs[:7], refs[7:]
    (keys, pre_low, low_grad), grads, (held, copied) = refs[:3], refs[3:-2], refs[-2:]
    projected = own[...] + received[...]
    rows, width = projected.shape
    gains = gain[...]
    slots, counts = told[:, :1], told[:, 1:2]
    adapter_total = jnp.sum(jnp.where(slots == slots[:1], counts, 0.0), axis=0, keepdims=True)
    live = lax.broadcasted_iota(jnp.int32, (rows, 1), 0).astype(F32) < counts[:1]
    weight = rows / jnp.broadcast_to(adapter_total, (rows, 1))
    weight = jnp.where(live, weight, 0.0)
    heads = []
    for head in range(width // HD):
        columns = slice(head * HD, (head + 1) * HD)
        values = projected[:, columns]
        inverse = lax.rsqrt(jnp.mean(values * values, axis=-1, keepdims=True) + norm_eps)
        normed = values * inverse
        held[:, columns] = (normed * gains).astype(BF16)
        scaled = cotangent[:, columns].astype(F32) * weight * gains
        along = jnp.mean(scaled * normed, axis=-1, keepdims=True)
        heads.append(inverse * (scaled - normed * along))
    copy = pltpu.make_async_copy(held, keys, copied)
    copy.start()
    pre = jnp.concatenate(heads, axis=-1)
    pre_low[...] = pre.astype(BF16)
    (pre_high, pre_rest), (up_high, up_rest), (low_high, low_rest) = map(split_two, (pre, up[...], low_rank[...]))
    rank = up.shape[0]
    both = lax.dot_general(
        jnp.concatenate([pre_high, pre_rest], axis=0),
        jnp.concatenate([up_high, up_rest], axis=0),
        (((1,), (1,)), ((), ())),
        preferred_element_type=F32,
    )
    grad = adapter_scale * (both[:rows, :rank] + both[:rows, rank:] + both[rows:, :rank])
    low_grad[...] = grad
    across = (((0,), (0,)), ((), ()))
    both = lax.dot_general(
        jnp.concatenate([low_high, low_rest], axis=-1), pre_high, across, preferred_element_type=F32
    )
    rest = lax.dot_general(low_high, pre_rest, across, preferred_element_type=F32)
    up_grad = adapter_scale * (both[:rank] + both[rank:] + rest)
    split = jnp.concatenate(split_two(grad), axis=-1)
    down_width, up_width = tokens.shape[1] // parts, width // parts
    for partner, out in enumerate(grads):
        part = place[0] ^ partner
        columns = pl.ds(pl.multiple_of(part * down_width, 128), down_width)
        both = lax.dot_general(split, tokens[:, columns], (((0,), (0,)), ((), ())), preferred_element_type=F32)
        out[:, :down_width] = (both[:rank] + both[rank:]).astype(out.dtype)
        for other in range(parts):

            @pl.when(part == other)
            def _():
                out[:, down_width:] = up_grad[:, other * up_width : (other + 1) * up_width].astype(out.dtype)
    copy.wait()


def input_grad_kernel(pieces, sizes, pre_low, low_grad, split, *refs):
    place = position()
    buffers, (out, held, copied) = refs[:-3], refs[-3:]
    rank = low_grad.shape[1]
    high, low = split_two(low_grad[...])
    left = jnp.concatenate([high, high, low], axis=-1)
    turned = pre_low[...].T
    copies = []
    for index, piece in enumerate(pieces):
        columns = pl.ds(column_of(place, piece, *sizes), piece["rows"])
        rows = pl.ds(piece["first"], piece["rows"])
        value = jnp.dot(buffers[piece["buffer"]][rows, :], turned, preferred_element_type=F32).T
        right = jnp.concatenate([split[:, columns], split[:rank, columns]], axis=0)
        value = value + jnp.dot(left, right, preferred_element_type=F32)
        held[:, columns] = value.astype(BF16)
        copies.append(pltpu.make_async_copy(held.at[:, columns], out.at[:, columns], copied.at[index]))
        copies[-1].start()
    for copy in copies:
        copy.wait()


def sum_kernel(told, *refs):
    grads, (down, up, down_held, up_held, copied) = refs[:-5], refs[-5:]
    width = down.shape[2]
    copies = []
    for stored in range(down.shape[0]):
        total = jnp.zeros(grads[0].shape, F32)
        for partner, grad in enumerate(grads):
            slot = told[partner : partner + 1, :1]
            total = total + jnp.where(slot == stored, grad[...].astype(F32), 0.0)
        down_held[stored] = total[:, :width]
        up_held[stored] = total[:, width:]
        for source, target in ((down_held, down), (up_held, up)):
            copies.append(pltpu.make_async_copy(source.at[stored], target.at[stored], copied.at[len(copies)]))
            copies[-1].start()
    for copy in copies:
        copy.wait()


def ordered(value, *earlier):
    return lax.optimization_barrier((value, *earlier))[0]


def flip(value, axis, size, bits):
    return lax.ppermute(value, axis, [(i, i ^ bits) for i in range(size)])


def on_device_lines(
    sizes,
    tokens,
    frozen_key_matrix,
    adapter_down_factor,
    adapter_up_factor,
    key_norm_gain,
    adapter_offset,
    loss_row_count,
    cotangent,
):
    parts, shards = sizes
    rows, model_width = tokens.shape
    key_width = frozen_key_matrix.shape[1]
    stored, down_width, rank = adapter_down_factor.shape
    up_width = adapter_up_factor.shape[2]
    shard_rows = frozen_key_matrix.shape[0]
    part_rows = shard_rows // parts
    over_dp = lambda value, bits: flip(value, "dp", parts, bits)
    over_z = lambda value, bits: flip(value, "fsdp", shards, bits * CORES)
    over_core = lambda value: flip(value, "fsdp", shards, 1)

    def over_split(value, dp_bits, z_bits):
        pairs = []
        for i in range(parts):
            for j in range(shards):
                core = j % CORES
                pairs.append((i * shards + j, (i ^ dp_bits[core]) * shards + (j ^ (z_bits[core] * CORES))))
        return lax.ppermute(value, ("dp", "fsdp"), pairs)

    near_both = (CORES * part_rows, key_width)

    def joined(*values):
        rows = len(values) * part_rows
        outs = [((rows, key_width), BF16)]
        return call(functools.partial(join_kernel, part_rows), outs, [(vmem, value) for value in values], "join")[0]

    matrix = frozen_key_matrix
    part = ((part_rows, key_width), BF16)
    (near,) = call(functools.partial(part_kernel, 0), [part], [(vmem, matrix)], "near")
    z2, z1 = over_z(near, 2), over_z(near, 1)
    (info,) = call(info_kernel, [((1, HD), F32)], [(vmem, adapter_offset)], "info")
    offsets = [info] + [over_dp(info, bits) for bits in range(1, parts)]
    held = call(
        hold_kernel,
        [((1, HD), F32), ((stored, rank, down_width), F32), (adapter_up_factor.shape, F32)],
        [(vmem, loss_row_count), (vmem, jnp.swapaxes(adapter_down_factor, 1, 2)), (vmem, adapter_up_factor)],
        "hold",
    )
    offsets, held = lax.optimization_barrier((offsets, held))
    wide = down_width + up_width + HD
    slots, own, sooner, later = call(
        messages_kernel,
        [((parts, HD), F32), ((rank, wide), F32), ((2 * rank, wide), F32), ((rank, wide), F32)],
        [(vmem, value) for value in (*offsets, *held)],
        "adapter_messages",
    )
    z2, z1 = ordered((z2, z1), sooner)
    sooner = over_split(sooner, (1, 2), (0, 0))
    z3 = over_z(z2, 1)
    z1_pair, z2_pair, sooner = lax.optimization_barrier((over_core(z1), over_core(z2), sooner))
    m12 = joined(z1, z1_pair, z2, z2_pair)
    xy12 = over_split(m12, (1, 2), (0, 0))
    matrix_pair, tokens_pair = over_core(ordered(matrix, m12)), over_core(ordered(tokens, m12))
    z3, matrix_pair, tokens_pair = lax.optimization_barrier((z3, matrix_pair, tokens_pair))
    (onward,) = call(pass_on_kernel, [((2 * rank, wide), F32)], [(vmem, later), (vmem, sooner)], "pass_on")
    later = over_split(onward, (2, 1), (0, 0))
    m3 = joined(z3, over_core(z3))
    xy3 = over_split(m3, (1, 2), (0, 0))
    (fars,) = call(
        functools.partial(part_kernel, parts - 1), [(near_both, BF16)], [(vmem, matrix), (vmem, matrix_pair)], "far"
    )
    d13 = over_split(ordered(fars, z3), (0, 0), (1, 3))
    xy12 = ordered(xy12, m3)
    (m4,) = call(functools.partial(take_kernel, part_rows, (2,)), [part], [(vmem, xy12)], "take")
    xy4 = over_split(m4, (2, 1), (0, 0))

    def piece(z, dp_bits, core, count=part_rows, first=0):
        pair = lambda value: value if isinstance(value, tuple) else (value, value)
        dp_bits = None if dp_bits is None else pair(dp_bits)
        return dict(z=pair(z), dp=dp_bits, core=core, rows=count, first=first)

    def two(z, dp_bits, core=0, first=0):
        return [piece(z, dp_bits, core, first=first), piece(z, dp_bits, 1 - core, first=first + part_rows)]

    def flat(batch):
        buffers = [value for value, _ in batch]
        pieces = [dict(item, buffer=index) for index, (_, items) in enumerate(batch) for item in items]
        return buffers, pieces

    def base(before, shared, alone):
        buffers, pieces = flat(shared + alone)
        mine = [item for item in pieces if item["buffer"] < len(shared)]
        lone = [item for item in pieces if item["buffer"] >= len(shared)]
        return call(
            functools.partial(base_kernel, mine, lone, (part_rows, parts)),
            [((rows, key_width), F32)] * 2,
            [(vmem, value) for value in (tokens, tokens_pair, *before, *buffers)],
            "base",
        )

    split, up, low_rank, total, told = call(
        low_rank_kernel,
        [
            ((2 * rank, model_width), BF16),
            ((rank, key_width), F32),
            ((rows, rank), F32),
            ((rows, key_width), F32),
            ((parts, HD), F32),
        ],
        [(vmem, value) for value in (tokens, slots, own, sooner, later)],
        "low_rank",
        moved=12 * 2**20,
    )
    last = CORES * part_rows
    shared = [
        (matrix, [piece(0, None, 0, shard_rows)]),
        (matrix_pair, [piece(0, None, 1, shard_rows)]),
        (m12, two(1, 0) + two(2, 0, 0, last)),
        (m3, two(3, 0)),
    ]
    early = [(xy12, two(1, (1, 2)) + two(2, (1, 2), 0, last))]
    totals = base((total, jnp.zeros_like(total)), shared, early)
    xy12, xy3, xy4, d13, totals = lax.optimization_barrier((xy12, xy3, xy4, d13, totals))
    late = [(xy3, two(3, (1, 2))), (d13, two((1, 3), 3)), (xy4, [piece(2, 3, 0)])]
    total, total_pair = base(totals, [], late)
    received = over_core(total_pair)
    lone = call(
        functools.partial(join_kernel, None),
        [((5 * part_rows, key_width), BF16)],
        [(vmem, value) for value in (xy3, d13, xy4)],
        "join",
    )[0]
    xy12_pair, lone_pair = over_core(ordered(xy12, received)), over_core(ordered(lone, received))
    keys, pre_low, low_grad, *grads = call(
        functools.partial(middle_kernel, parts),
        [((rows, key_width), BF16), ((rows, key_width), BF16), ((rows, rank), F32)]
        + [((rank, down_width + up_width), F32)]
        + [((rank, down_width + up_width), BF16)] * (parts - 1),
        [
            (vmem, value)
            for value in (told, tokens, total, received, cotangent, key_norm_gain.reshape(1, HD), low_rank, up)
        ],
        "key_norm",
        out=[hbm] + [vmem] * (2 + parts),
        scratch=[pltpu.VMEM((rows, key_width), BF16), pltpu.SemaphoreType.DMA],
    )
    others = [
        (xy12_pair, two(1, (2, 1), 1) + two(2, (2, 1), 1, last)),
        (lone_pair, two(3, (2, 1), 1) + two((3, 1), 3, 1, last) + [piece(2, 3, 1, first=2 * last)]),
    ]
    received = [grads[0]] + [over_dp(grads[bits], bits) for bits in range(1, parts)]
    buffers, pieces = flat(shared + early + late + others)
    (input_grad,) = call(
        functools.partial(input_grad_kernel, pieces, (part_rows, parts)),
        [((rows, model_width), BF16)],
        [(vmem, pre_low), (vmem, low_grad), (vmem, split)] + [(vmem, value) for value in buffers],
        "input_grad",
        out=hbm,
        scratch=[pltpu.VMEM((rows, model_width), BF16), pltpu.SemaphoreType.DMA((len(pieces),))],
    )
    received, input_grad = lax.optimization_barrier((received, input_grad))
    down_sum, up_sum = call(
        sum_kernel,
        [((stored, rank, down_width), F32), ((stored, rank, up_width), F32)],
        [(vmem, told)] + [(vmem, value) for value in received],
        "grad_sum",
        out=hbm,
        scratch=[
            pltpu.VMEM((stored, rank, down_width), F32),
            pltpu.VMEM((stored, rank, up_width), F32),
            pltpu.SemaphoreType.DMA((2 * stored,)),
        ],
    )
    return keys, input_grad, jnp.swapaxes(down_sum, 1, 2), up_sum


def on_device_any(
    tokens,
    frozen_key_matrix,
    adapter_down_factor,
    adapter_up_factor,
    key_norm_gain,
    adapter_offset,
    loss_row_count,
    cotangent,
):
    row_count = tokens.shape[0]
    key_width = frozen_key_matrix.shape[1]
    stored_values = adapter_down_factor.shape[0]
    slot_value = adapter_offset[0, 0]
    live_count = loss_row_count[0, 0]
    selector = jnp.arange(stored_values, dtype=jnp.int32) == slot_value
    counted = jnp.where(selector, live_count, 0)
    summed_rows = lax.psum(counted, "dp")
    adapter_total = jnp.sum(jnp.where(selector, summed_rows, 0)).astype(F32)
    down_whole = lax.all_gather(adapter_down_factor, "dp", axis=1, tiled=True)
    up_whole = lax.all_gather(adapter_up_factor, "dp", axis=2, tiled=True)
    down_projection = lax.dynamic_index_in_dim(down_whole, slot_value, 0, keepdims=False)
    up_projection = lax.dynamic_index_in_dim(up_whole, slot_value, 0, keepdims=False)
    weight = lax.all_gather(frozen_key_matrix, "fsdp", axis=0, tiled=True)
    frozen_output = jnp.dot(tokens, weight, preferred_element_type=F32)
    tokens_float = tokens.astype(F32)
    lowrank_output = jnp.dot(tokens_float, down_projection, precision=HIGHEST)
    projected_keys = frozen_output + adapter_scale * jnp.dot(lowrank_output, up_projection, precision=HIGHEST)
    shaped = projected_keys.reshape(row_count, -1, HD)
    mean_square = jnp.mean(shaped * shaped, axis=-1, keepdims=True)
    inverse_rms = lax.rsqrt(mean_square + norm_eps)
    normed = shaped * inverse_rms
    keys = (normed * key_norm_gain).reshape(row_count, key_width).astype(BF16)
    row_mask = (jnp.arange(row_count, dtype=jnp.int32) < live_count).astype(F32)
    row_grad = cotangent.astype(F32) * row_mask[:, None] * (row_count / adapter_total)
    scaled_grad = row_grad.reshape(normed.shape) * key_norm_gain
    along_norm = jnp.mean(scaled_grad * normed, axis=-1, keepdims=True)
    prenorm_gradient = (inverse_rms * (scaled_grad - normed * along_norm)).reshape(row_count, key_width)
    pre_grad_low = prenorm_gradient.astype(BF16)
    lowrank_gradient = adapter_scale * jnp.dot(prenorm_gradient, up_projection.T, precision=HIGHEST)
    input_base = lax.dot_general(pre_grad_low, weight, (((1,), (1,)), ((), ())), preferred_element_type=F32)
    input_grad = (input_base + jnp.dot(lowrank_gradient, down_projection.T, precision=HIGHEST)).astype(BF16)
    down_grad = lax.dot_general(tokens_float, lowrank_gradient, (((0,), (0,)), ((), ())), precision=HIGHEST)
    up_factor_gradient = adapter_scale * lax.dot_general(
        lowrank_output, prenorm_gradient, (((0,), (0,)), ((), ())), precision=HIGHEST
    )
    selector_float = selector.astype(F32)
    down_terms = selector_float[:, None, None] * down_grad[None]
    up_terms = selector_float[:, None, None] * up_factor_gradient[None]
    down_sum = lax.psum_scatter(down_terms, "dp", scatter_dimension=1, tiled=True)
    up_sum = lax.psum_scatter(up_terms, "dp", scatter_dimension=2, tiled=True)
    return keys, input_grad, down_sum, up_sum


def solution(mesh):
    placed = (
        P(("dp", "fsdp"), None),
        P("fsdp", None),
        P("fsdp", "dp", None),
        P("fsdp", None, "dp"),
        P(),
        P("dp", "fsdp"),
        P("dp", "fsdp"),
        P(("dp", "fsdp"), None),
    )
    sizes = mesh.shape["dp"], mesh.shape["fsdp"]
    lines = sizes == (4, 4 * CORES)
    return jax.shard_map(
        functools.partial(on_device_lines, sizes) if lines else on_device_any,
        mesh=mesh,
        in_specs=placed,
        out_specs=(
            P(("dp", "fsdp"), None),
            P(("dp", "fsdp"), None),
            P("fsdp", "dp", None),
            P("fsdp", None, "dp"),
        ),
        check_vma=False,
    )
```

```python
import functools

import jax
import jax.numpy as jnp
from jax import lax
from jax.experimental import pallas as pl
from jax.experimental.pallas import tpu as pltpu
from jax.sharding import PartitionSpec as P

HD = 128
CORES = 2

adapter_scale = 2.0
norm_eps = 1e-06

F32 = jnp.float32
BF16 = jnp.bfloat16
HIGHEST = lax.Precision.HIGHEST
VMEM_LIMIT = 8 * 2**20

vmem = pl.BlockSpec(memory_space=pltpu.VMEM)
smem = pl.BlockSpec(memory_space=pltpu.SMEM)
hbm = pl.BlockSpec(memory_space=pltpu.HBM)


def split_two(value):
    high = value.astype(BF16)
    low = (value - high.astype(F32)).astype(BF16)
    return high, low


def call(kernel, outs, ins, name, moved=0, out=vmem, scratch=()):
    return pl.pallas_call(
        kernel,
        out_shape=[jax.ShapeDtypeStruct(shape, dtype) for shape, dtype in outs],
        in_specs=[spec for spec, _ in ins],
        out_specs=out if isinstance(out, list) else [out] * len(outs),
        scratch_shapes=scratch,
        compiler_params=pltpu.CompilerParams(vmem_limit_bytes=VMEM_LIMIT),
        cost_estimate=pl.CostEstimate(flops=0, bytes_accessed=moved, transcendentals=0),
        name=name,
    )(*[value for _, value in ins])


def position():
    fsdp = lax.axis_index("fsdp")
    return lax.axis_index("dp"), lax.div(fsdp, CORES), lax.rem(fsdp, CORES)


def part_kernel(bits, *refs):
    out = refs[-1]
    rows = out.shape[0] // (len(refs) - 1)
    part = lax.axis_index("dp") ^ bits
    for index, matrix in enumerate(refs[:-1]):
        out[index * rows : (index + 1) * rows] = matrix[pl.ds(pl.multiple_of(part * rows, rows), rows), :]


def info_kernel(offset, info):
    info[...] = jnp.broadcast_to(offset[...].astype(F32), info.shape)


def hold_kernel(count, down, up, count_held, down_held, up_held):
    count_held[...] = jnp.broadcast_to(count[...].astype(F32), count_held.shape)
    down_held[...] = down[...]
    up_held[...] = up[...]


def chosen(stored, slot):
    return sum(jnp.where(slot == index, stored[index], 0.0) for index in range(stored.shape[0]))


def messages_kernel(*refs):
    parts = len(refs) - 7
    offsets, (count, down, up), (slots, own, sooner, later) = refs[:parts], refs[parts : parts + 3], refs[parts + 3 :]
    rank, width = down.shape[1], down.shape[2]
    wide = width + up.shape[2]
    first_core = position()[2] == 0
    for partner, offset in enumerate(offsets):
        slots[partner : partner + 1, :] = offset[...]
    near, side, beside, far = (offset[:, :1] for offset in offsets)
    wanted = jnp.where(first_core, side, beside), jnp.where(first_core, beside, side)
    for slot, out, first in ((near, own, 0), (wanted[0], sooner, 0), (wanted[1], later, 0), (far, sooner, rank)):
        rows = pl.ds(first, rank)
        out[rows, :width] = chosen(down, slot)
        out[rows, width:wide] = chosen(up, slot)
        out[rows, wide:] = jnp.broadcast_to(count[...], (rank, HD))


def pass_on_kernel(later, received, out):
    rank = later.shape[0]
    out[:rank] = later[...]
    out[rank:] = received[rank:]


def take_kernel(each, wanted, value, out):
    for index, place in enumerate(wanted):
        out[index * each : (index + 1) * each] = value[place * each : (place + 1) * each]


def join_kernel(each, *refs):
    out, first = refs[-1], 0
    for ref in refs[:-1]:
        rows = each or ref.shape[0]
        out[first : first + rows] = ref[:rows]
        first += rows


def low_rank_kernel(tokens, slots, own, sooner, later, split, up, low_rank, total, told):
    rank = low_rank.shape[1]
    messages = own, sooner.at[:rank], later.at[:rank], later.at[rank:]
    parts = len(messages)
    down_width = tokens.shape[1] // parts
    up_width = up.shape[1] // parts
    dp, _, core = position()
    lane = lax.broadcasted_iota(jnp.int32, (1, HD), 1)
    counts = [message[:1, down_width + up_width :] for message in messages]
    counts[1:3] = jnp.where(core == 0, counts[1], counts[2]), jnp.where(core == 0, counts[2], counts[1])
    for partner, count in enumerate(counts):
        told[partner : partner + 1, :] = jnp.where(lane == 0, slots[partner : partner + 1, :], count)
    partners = 0, jnp.where(core == 0, 1, 2), jnp.where(core == 0, 2, 1), 3
    for partner, message in zip(partners, messages):
        part = dp ^ partner
        columns = pl.ds(pl.multiple_of(part * down_width, 128), down_width)
        high, low = split_two(message[:, :down_width])
        split[:rank, columns] = high
        split[rank:, columns] = low
        columns = pl.ds(pl.multiple_of(part * up_width, 128), up_width)
        up[:, columns] = message[:, down_width : down_width + up_width]
    both = lax.dot_general(tokens[...], split[...], (((1,), (1,)), ((), ())), preferred_element_type=F32)
    low_rank[...] = both[:, :rank] + both[:, rank:]
    total[...] = adapter_scale * jnp.dot(low_rank[...], up[...], precision=HIGHEST, preferred_element_type=F32)


def by_core(place, value):
    first, second = value
    return first if first == second else jnp.where(place[2] == 0, first, second)


def column_of(place, piece, part_rows, parts):
    shard = (place[1] ^ by_core(place, piece["z"])) * CORES + (place[2] ^ piece["core"])
    part = 0 if piece["dp"] is None else place[0] ^ by_core(place, piece["dp"])
    return pl.multiple_of((shard * parts + part) * part_rows, 128)


def base_sum(place, rows, total, buffers, pieces, sizes):
    for piece in pieces:
        columns = pl.ds(column_of(place, piece, *sizes), piece["rows"])
        part = pl.ds(piece["first"], piece["rows"])
        left = jnp.concatenate([ref[:, columns] for ref in rows], axis=0) if len(rows) > 1 else rows[0][:, columns]
        value = jnp.dot(left, buffers[piece["buffer"]][part, :], preferred_element_type=F32)
        total = value if total is None else total + value
    return total


def base_kernel(pieces, alone, sizes, tokens, tokens_pair, before, before_pair, *refs):
    place = position()
    buffers, (total, total_pair) = refs[:-2], refs[-2:]
    count = tokens.shape[0]
    both = base_sum(place, (tokens, tokens_pair), None, buffers, alone, sizes)
    total[...] = base_sum(place, (tokens,), before[...] + both[:count], buffers, pieces, sizes)
    total_pair[...] = before_pair[...] + both[count:]


def middle_kernel(parts, told, *refs):
    place = position()
    (tokens, own, received, cotangent, gain, low_rank, up), refs = refs[:7], refs[7:]
    (keys, pre_low, low_grad), grads, (held, copied) = refs[:3], refs[3:-2], refs[-2:]
    projected = own[...] + received[...]
    rows, width = projected.shape
    gains = gain[...]
    slots, counts = told[:, :1], told[:, 1:2]
    adapter_total = jnp.sum(jnp.where(slots == slots[:1], counts, 0.0), axis=0, keepdims=True)
    live = lax.broadcasted_iota(jnp.int32, (rows, 1), 0).astype(F32) < counts[:1]
    weight = rows / jnp.broadcast_to(adapter_total, (rows, 1))
    weight = jnp.where(live, weight, 0.0)
    heads = []
    for head in range(width // HD):
        columns = slice(head * HD, (head + 1) * HD)
        values = projected[:, columns]
        inverse = lax.rsqrt(jnp.mean(values * values, axis=-1, keepdims=True) + norm_eps)
        normed = values * inverse
        held[:, columns] = (normed * gains).astype(BF16)
        scaled = cotangent[:, columns].astype(F32) * weight * gains
        along = jnp.mean(scaled * normed, axis=-1, keepdims=True)
        heads.append(inverse * (scaled - normed * along))
    copy = pltpu.make_async_copy(held, keys, copied)
    copy.start()
    pre = jnp.concatenate(heads, axis=-1)
    pre_low[...] = pre.astype(BF16)
    (pre_high, pre_rest), (up_high, up_rest), (low_high, low_rest) = map(split_two, (pre, up[...], low_rank[...]))
    rank = up.shape[0]
    both = lax.dot_general(
        jnp.concatenate([pre_high, pre_rest], axis=0),
        jnp.concatenate([up_high, up_rest], axis=0),
        (((1,), (1,)), ((), ())),
        preferred_element_type=F32,
    )
    grad = adapter_scale * (both[:rows, :rank] + both[:rows, rank:] + both[rows:, :rank])
    low_grad[...] = grad
    across = (((0,), (0,)), ((), ()))
    both = lax.dot_general(
        jnp.concatenate([low_high, low_rest], axis=-1), pre_high, across, preferred_element_type=F32
    )
    rest = lax.dot_general(low_high, pre_rest, across, preferred_element_type=F32)
    up_grad = adapter_scale * (both[:rank] + both[rank:] + rest)
    split = jnp.concatenate(split_two(grad), axis=-1)
    down_width, up_width = tokens.shape[1] // parts, width // parts
    for partner, out in enumerate(grads):
        part = place[0] ^ partner
        columns = pl.ds(pl.multiple_of(part * down_width, 128), down_width)
        both = lax.dot_general(split, tokens[:, columns], (((0,), (0,)), ((), ())), preferred_element_type=F32)
        out[:, :down_width] = (both[:rank] + both[rank:]).astype(out.dtype)
        for other in range(parts):

            @pl.when(part == other)
            def _():
                out[:, down_width:] = up_grad[:, other * up_width : (other + 1) * up_width].astype(out.dtype)
    copy.wait()


def input_grad_kernel(pieces, sizes, pre_low, low_grad, split, *refs):
    place = position()
    buffers, (out, held, copied) = refs[:-3], refs[-3:]
    rank = low_grad.shape[1]
    high, low = split_two(low_grad[...])
    left = jnp.concatenate([high, high, low], axis=-1)
    turned = pre_low[...].T
    copies = []
    for index, piece in enumerate(pieces):
        if index == 0 or piece["buffer"] != pieces[index - 1]["buffer"]:
            whole = jnp.dot(buffers[piece["buffer"]][...], turned, preferred_element_type=F32).T
        columns = pl.ds(column_of(place, piece, *sizes), piece["rows"])
        right = jnp.concatenate([split[:, columns], split[:rank, columns]], axis=0)
        value = whole[:, piece["first"] : piece["first"] + piece["rows"]]
        value = value + jnp.dot(left, right, preferred_element_type=F32)
        held[:, columns] = value.astype(BF16)
        copies.append(pltpu.make_async_copy(held.at[:, columns], out.at[:, columns], copied.at[index]))
        copies[-1].start()
    for copy in copies:
        copy.wait()


def sum_kernel(told, *refs):
    grads, (down, up, down_held, up_held, copied) = refs[:-5], refs[-5:]
    width = down.shape[2]
    copies = []
    for stored in range(down.shape[0]):
        total = jnp.zeros(grads[0].shape, F32)
        for partner, grad in enumerate(grads):
            slot = told[partner : partner + 1, :1]
            total = total + jnp.where(slot == stored, grad[...].astype(F32), 0.0)
        down_held[stored] = total[:, :width]
        up_held[stored] = total[:, width:]
        for source, target in ((down_held, down), (up_held, up)):
            copies.append(pltpu.make_async_copy(source.at[stored], target.at[stored], copied.at[len(copies)]))
            copies[-1].start()
    for copy in copies:
        copy.wait()


def ordered(value, *earlier):
    return lax.optimization_barrier((value, *earlier))[0]


def flip(value, axis, size, bits):
    return lax.ppermute(value, axis, [(i, i ^ bits) for i in range(size)])


def on_device_lines(
    sizes,
    tokens,
    frozen_key_matrix,
    adapter_down_factor,
    adapter_up_factor,
    key_norm_gain,
    adapter_offset,
    loss_row_count,
    cotangent,
):
    parts, shards = sizes
    rows, model_width = tokens.shape
    key_width = frozen_key_matrix.shape[1]
    stored, down_width, rank = adapter_down_factor.shape
    up_width = adapter_up_factor.shape[2]
    shard_rows = frozen_key_matrix.shape[0]
    part_rows = shard_rows // parts
    over_dp = lambda value, bits: flip(value, "dp", parts, bits)
    over_z = lambda value, bits: flip(value, "fsdp", shards, bits * CORES)
    over_core = lambda value: flip(value, "fsdp", shards, 1)

    def over_split(value, dp_bits, z_bits):
        pairs = []
        for i in range(parts):
            for j in range(shards):
                core = j % CORES
                pairs.append((i * shards + j, (i ^ dp_bits[core]) * shards + (j ^ (z_bits[core] * CORES))))
        return lax.ppermute(value, ("dp", "fsdp"), pairs)

    near_both = (CORES * part_rows, key_width)

    def joined(*values):
        rows = len(values) * part_rows
        outs = [((rows, key_width), BF16)]
        return call(functools.partial(join_kernel, part_rows), outs, [(vmem, value) for value in values], "join")[0]

    matrix = frozen_key_matrix
    part = ((part_rows, key_width), BF16)
    near = lax.dynamic_slice_in_dim(matrix, lax.axis_index("dp") * part_rows, part_rows, 0)
    z1, z2 = over_z(near, 1), over_z(near, 2)
    (info,) = call(info_kernel, [((1, HD), F32)], [(vmem, adapter_offset)], "info")
    offsets = [info] + [over_dp(info, bits) for bits in range(1, parts)]
    held = call(
        hold_kernel,
        [((1, HD), F32), ((stored, rank, down_width), F32), (adapter_up_factor.shape, F32)],
        [(vmem, loss_row_count), (vmem, jnp.swapaxes(adapter_down_factor, 1, 2)), (vmem, adapter_up_factor)],
        "hold",
    )
    offsets, held = lax.optimization_barrier((offsets, held))
    wide = down_width + up_width + HD
    slots, own, sooner, later = call(
        messages_kernel,
        [((parts, HD), F32), ((rank, wide), F32), ((2 * rank, wide), F32), ((rank, wide), F32)],
        [(vmem, value) for value in (*offsets, *held)],
        "adapter_messages",
    )
    z1, z2 = ordered((z1, z2), sooner)
    sooner = over_split(sooner, (1, 2), (0, 0))
    z3 = over_z(z2, 1)
    z1_pair, z2_pair, sooner = lax.optimization_barrier((over_core(z1), over_core(z2), sooner))
    m12 = joined(z1, z1_pair, z2, z2_pair)
    xy12 = over_split(m12, (1, 2), (0, 0))
    matrix_pair, tokens_pair = over_core(ordered(matrix, m12)), over_core(ordered(tokens, m12))
    z3, matrix_pair, tokens_pair = lax.optimization_barrier((z3, matrix_pair, tokens_pair))
    (onward,) = call(pass_on_kernel, [((2 * rank, wide), F32)], [(vmem, later), (vmem, sooner)], "pass_on")
    later = over_split(onward, (2, 1), (0, 0))
    m3 = joined(z3, over_core(z3))
    xy3 = over_split(m3, (1, 2), (0, 0))
    (fars,) = call(
        functools.partial(part_kernel, parts - 1), [(near_both, BF16)], [(vmem, matrix), (vmem, matrix_pair)], "far"
    )
    d13 = over_split(ordered(fars, z3), (0, 0), (1, 3))
    xy12 = ordered(xy12, m3)
    (m4,) = call(functools.partial(take_kernel, part_rows, (2,)), [part], [(vmem, xy12)], "take")
    xy4 = over_split(m4, (2, 1), (0, 0))

    def piece(z, dp_bits, core, count=part_rows, first=0):
        pair = lambda value: value if isinstance(value, tuple) else (value, value)
        dp_bits = None if dp_bits is None else pair(dp_bits)
        return dict(z=pair(z), dp=dp_bits, core=core, rows=count, first=first)

    def two(z, dp_bits, core=0, first=0):
        return [piece(z, dp_bits, core, first=first), piece(z, dp_bits, 1 - core, first=first + part_rows)]

    def flat(batch):
        buffers = [value for value, _ in batch]
        pieces = [dict(item, buffer=index) for index, (_, items) in enumerate(batch) for item in items]
        return buffers, pieces

    def base(before, shared, alone):
        buffers, pieces = flat(shared + alone)
        mine = [item for item in pieces if item["buffer"] < len(shared)]
        lone = [item for item in pieces if item["buffer"] >= len(shared)]
        return call(
            functools.partial(base_kernel, mine, lone, (part_rows, parts)),
            [((rows, key_width), F32)] * 2,
            [(vmem, value) for value in (tokens, tokens_pair, *before, *buffers)],
            "base",
        )

    split, up, low_rank, total, told = call(
        low_rank_kernel,
        [
            ((2 * rank, model_width), BF16),
            ((rank, key_width), F32),
            ((rows, rank), F32),
            ((rows, key_width), F32),
            ((parts, HD), F32),
        ],
        [(vmem, value) for value in (tokens, slots, own, sooner, later)],
        "low_rank",
        moved=12 * 2**20,
    )
    last = CORES * part_rows
    shared = [
        (matrix, [piece(0, None, 0, shard_rows)]),
        (matrix_pair, [piece(0, None, 1, shard_rows)]),
        (m12, two(1, 0) + two(2, 0, 0, last)),
        (m3, two(3, 0)),
    ]
    early = [(xy12, two(1, (1, 2)) + two(2, (1, 2), 0, last))]
    totals = base((total, jnp.zeros_like(total)), shared, early)
    xy12, xy3, xy4, d13, totals = lax.optimization_barrier((xy12, xy3, xy4, d13, totals))
    late = [(xy3, two(3, (1, 2))), (d13, two((1, 3), 3)), (xy4, [piece(2, 3, 0)])]
    total, total_pair = base(totals, [], late)
    received = over_core(total_pair)
    (lone,) = call(
        functools.partial(join_kernel, None),
        [((9 * part_rows, key_width), BF16)],
        [(vmem, value) for value in (xy12, xy3, d13, xy4)],
        "join",
    )
    lone_pair = over_core(ordered(lone, received))
    keys, pre_low, low_grad, *grads = call(
        functools.partial(middle_kernel, parts),
        [((rows, key_width), BF16), ((rows, key_width), BF16), ((rows, rank), F32)]
        + [((rank, down_width + up_width), F32)]
        + [((rank, down_width + up_width), BF16)] * (parts - 1),
        [
            (vmem, value)
            for value in (told, tokens, total, received, cotangent, key_norm_gain.reshape(1, HD), low_rank, up)
        ],
        "key_norm",
        out=[hbm] + [vmem] * (2 + parts),
        scratch=[pltpu.VMEM((rows, key_width), BF16), pltpu.SemaphoreType.DMA],
    )
    others = two(1, (2, 1), 1) + two(2, (2, 1), 1, last) + two(3, (2, 1), 1, 2 * last) + two((3, 1), 3, 1, 3 * last)
    others = [(lone_pair, others + [piece(2, 3, 1, first=4 * last)])]
    received = [grads[0]] + [over_dp(grads[bits], bits) for bits in range(1, parts)]
    buffers, pieces = flat(shared + early + late + others)
    (input_grad,) = call(
        functools.partial(input_grad_kernel, pieces, (part_rows, parts)),
        [((rows, model_width), BF16)],
        [(vmem, pre_low), (vmem, low_grad), (vmem, split)] + [(vmem, value) for value in buffers],
        "input_grad",
        out=hbm,
        scratch=[pltpu.VMEM((rows, model_width), BF16), pltpu.SemaphoreType.DMA((len(pieces),))],
    )
    received, input_grad = lax.optimization_barrier((received, input_grad))
    down_sum, up_sum = call(
        sum_kernel,
        [((stored, rank, down_width), F32), ((stored, rank, up_width), F32)],
        [(vmem, told)] + [(vmem, value) for value in received],
        "grad_sum",
        out=hbm,
        scratch=[
            pltpu.VMEM((stored, rank, down_width), F32),
            pltpu.VMEM((stored, rank, up_width), F32),
            pltpu.SemaphoreType.DMA((2 * stored,)),
        ],
    )
    return keys, input_grad, jnp.swapaxes(down_sum, 1, 2), up_sum


def on_device_any(
    tokens,
    frozen_key_matrix,
    adapter_down_factor,
    adapter_up_factor,
    key_norm_gain,
    adapter_offset,
    loss_row_count,
    cotangent,
):
    row_count = tokens.shape[0]
    key_width = frozen_key_matrix.shape[1]
    stored_values = adapter_down_factor.shape[0]
    slot_value = adapter_offset[0, 0]
    live_count = loss_row_count[0, 0]
    selector = jnp.arange(stored_values, dtype=jnp.int32) == slot_value
    counted = jnp.where(selector, live_count, 0)
    summed_rows = lax.psum(counted, "dp")
    adapter_total = jnp.sum(jnp.where(selector, summed_rows, 0)).astype(F32)
    down_whole = lax.all_gather(adapter_down_factor, "dp", axis=1, tiled=True)
    up_whole = lax.all_gather(adapter_up_factor, "dp", axis=2, tiled=True)
    down_projection = lax.dynamic_index_in_dim(down_whole, slot_value, 0, keepdims=False)
    up_projection = lax.dynamic_index_in_dim(up_whole, slot_value, 0, keepdims=False)
    weight = lax.all_gather(frozen_key_matrix, "fsdp", axis=0, tiled=True)
    frozen_output = jnp.dot(tokens, weight, preferred_element_type=F32)
    tokens_float = tokens.astype(F32)
    lowrank_output = jnp.dot(tokens_float, down_projection, precision=HIGHEST)
    projected_keys = frozen_output + adapter_scale * jnp.dot(lowrank_output, up_projection, precision=HIGHEST)
    shaped = projected_keys.reshape(row_count, -1, HD)
    mean_square = jnp.mean(shaped * shaped, axis=-1, keepdims=True)
    inverse_rms = lax.rsqrt(mean_square + norm_eps)
    normed = shaped * inverse_rms
    keys = (normed * key_norm_gain).reshape(row_count, key_width).astype(BF16)
    row_mask = (jnp.arange(row_count, dtype=jnp.int32) < live_count).astype(F32)
    row_grad = cotangent.astype(F32) * row_mask[:, None] * (row_count / adapter_total)
    scaled_grad = row_grad.reshape(normed.shape) * key_norm_gain
    along_norm = jnp.mean(scaled_grad * normed, axis=-1, keepdims=True)
    prenorm_gradient = (inverse_rms * (scaled_grad - normed * along_norm)).reshape(row_count, key_width)
    pre_grad_low = prenorm_gradient.astype(BF16)
    lowrank_gradient = adapter_scale * jnp.dot(prenorm_gradient, up_projection.T, precision=HIGHEST)
    input_base = lax.dot_general(pre_grad_low, weight, (((1,), (1,)), ((), ())), preferred_element_type=F32)
    input_grad = (input_base + jnp.dot(lowrank_gradient, down_projection.T, precision=HIGHEST)).astype(BF16)
    down_grad = lax.dot_general(tokens_float, lowrank_gradient, (((0,), (0,)), ((), ())), precision=HIGHEST)
    up_factor_gradient = adapter_scale * lax.dot_general(
        lowrank_output, prenorm_gradient, (((0,), (0,)), ((), ())), precision=HIGHEST
    )
    selector_float = selector.astype(F32)
    down_terms = selector_float[:, None, None] * down_grad[None]
    up_terms = selector_float[:, None, None] * up_factor_gradient[None]
    down_sum = lax.psum_scatter(down_terms, "dp", scatter_dimension=1, tiled=True)
    up_sum = lax.psum_scatter(up_terms, "dp", scatter_dimension=2, tiled=True)
    return keys, input_grad, down_sum, up_sum


def solution(mesh):
    placed = (
        P(("dp", "fsdp"), None),
        P("fsdp", None),
        P("fsdp", "dp", None),
        P("fsdp", None, "dp"),
        P(),
        P("dp", "fsdp"),
        P("dp", "fsdp"),
        P(("dp", "fsdp"), None),
    )
    sizes = mesh.shape["dp"], mesh.shape["fsdp"]
    lines = sizes == (4, 4 * CORES)
    return jax.shard_map(
        functools.partial(on_device_lines, sizes) if lines else on_device_any,
        mesh=mesh,
        in_specs=placed,
        out_specs=(
            P(("dp", "fsdp"), None),
            P(("dp", "fsdp"), None),
            P("fsdp", "dp", None),
            P("fsdp", None, "dp"),
        ),
        check_vma=False,
    )
```

```python
import functools

import jax
import jax.numpy as jnp
from jax import lax
from jax.experimental import pallas as pl
from jax.experimental.pallas import tpu as pltpu
from jax.sharding import PartitionSpec as P

HD = 128
CORES = 2

adapter_scale = 2.0
norm_eps = 1e-06

F32 = jnp.float32
BF16 = jnp.bfloat16
HIGHEST = lax.Precision.HIGHEST
VMEM_LIMIT = 8 * 2**20

vmem = pl.BlockSpec(memory_space=pltpu.VMEM)
smem = pl.BlockSpec(memory_space=pltpu.SMEM)
hbm = pl.BlockSpec(memory_space=pltpu.HBM)


def split_two(value):
    high = value.astype(BF16)
    low = (value - high.astype(F32)).astype(BF16)
    return high, low


def call(kernel, outs, ins, name, moved=0, out=vmem, scratch=()):
    return pl.pallas_call(
        kernel,
        out_shape=[jax.ShapeDtypeStruct(shape, dtype) for shape, dtype in outs],
        in_specs=[spec for spec, _ in ins],
        out_specs=out if isinstance(out, list) else [out] * len(outs),
        scratch_shapes=scratch,
        compiler_params=pltpu.CompilerParams(vmem_limit_bytes=VMEM_LIMIT),
        cost_estimate=pl.CostEstimate(flops=0, bytes_accessed=moved, transcendentals=0),
        name=name,
    )(*[value for _, value in ins])


def position():
    fsdp = lax.axis_index("fsdp")
    return lax.axis_index("dp"), lax.div(fsdp, CORES), lax.rem(fsdp, CORES)


def part_kernel(bits, *refs):
    out = refs[-1]
    rows = out.shape[0] // (len(refs) - 1)
    part = lax.axis_index("dp") ^ bits
    for index, matrix in enumerate(refs[:-1]):
        out[index * rows : (index + 1) * rows] = matrix[pl.ds(pl.multiple_of(part * rows, rows), rows), :]


def info_kernel(offset, info):
    info[...] = jnp.broadcast_to(offset[...].astype(F32), info.shape)


def hold_kernel(count, down, up, count_held, down_held, up_held):
    count_held[...] = jnp.broadcast_to(count[...].astype(F32), count_held.shape)
    down_held[...] = down[...]
    up_held[...] = up[...]


def chosen(stored, slot):
    return sum(jnp.where(slot == index, stored[index], 0.0) for index in range(stored.shape[0]))


def messages_kernel(*refs):
    parts = len(refs) - 7
    offsets, (count, down, up), (slots, own, sooner, later) = refs[:parts], refs[parts : parts + 3], refs[parts + 3 :]
    rank, width = down.shape[1], down.shape[2]
    wide = width + up.shape[2]
    first_core = position()[2] == 0
    for partner, offset in enumerate(offsets):
        slots[partner : partner + 1, :] = offset[...]
    near, side, beside, far = (offset[:, :1] for offset in offsets)
    wanted = jnp.where(first_core, side, beside), jnp.where(first_core, beside, side)
    for slot, out, first in ((near, own, 0), (wanted[0], sooner, 0), (wanted[1], later, 0), (far, sooner, rank)):
        rows = pl.ds(first, rank)
        out[rows, :width] = chosen(down, slot)
        out[rows, width:wide] = chosen(up, slot)
        out[rows, wide:] = jnp.broadcast_to(count[...], (rank, HD))


def pass_on_kernel(later, received, out):
    rank = later.shape[0]
    out[:rank] = later[...]
    out[rank:] = received[rank:]


def take_kernel(each, wanted, value, out):
    for index, place in enumerate(wanted):
        out[index * each : (index + 1) * each] = value[place * each : (place + 1) * each]


def join_kernel(each, *refs):
    out, first = refs[-1], 0
    for ref in refs[:-1]:
        rows = each or ref.shape[0]
        out[first : first + rows] = ref[:rows]
        first += rows


def low_rank_kernel(tokens, slots, own, sooner, later, split, up, low_rank, total, told):
    rank = low_rank.shape[1]
    messages = own, sooner.at[:rank], later.at[:rank], later.at[rank:]
    parts = len(messages)
    down_width = tokens.shape[1] // parts
    up_width = up.shape[1] // parts
    dp, _, core = position()
    lane = lax.broadcasted_iota(jnp.int32, (1, HD), 1)
    counts = [message[:1, down_width + up_width :] for message in messages]
    counts[1:3] = jnp.where(core == 0, counts[1], counts[2]), jnp.where(core == 0, counts[2], counts[1])
    for partner, count in enumerate(counts):
        told[partner : partner + 1, :] = jnp.where(lane == 0, slots[partner : partner + 1, :], count)
    partners = 0, jnp.where(core == 0, 1, 2), jnp.where(core == 0, 2, 1), 3
    for partner, message in zip(partners, messages):
        part = dp ^ partner
        columns = pl.ds(pl.multiple_of(part * down_width, 128), down_width)
        high, low = split_two(message[:, :down_width])
        split[:rank, columns] = high
        split[rank : 2 * rank, columns] = low
        split[2 * rank :, columns] = high
        columns = pl.ds(pl.multiple_of(part * up_width, 128), up_width)
        up[:, columns] = message[:, down_width : down_width + up_width]
    both = lax.dot_general(
        tokens[...], split[: 2 * rank, :], (((1,), (1,)), ((), ())), preferred_element_type=F32
    )
    low_rank[...] = both[:, :rank] + both[:, rank:]
    total[...] = adapter_scale * jnp.dot(low_rank[...], up[...], precision=HIGHEST, preferred_element_type=F32)


def by_core(place, value):
    first, second = value
    return first if first == second else jnp.where(place[2] == 0, first, second)


def column_of(place, piece, part_rows, parts):
    shard = (place[1] ^ by_core(place, piece["z"])) * CORES + (place[2] ^ piece["core"])
    part = 0 if piece["dp"] is None else place[0] ^ by_core(place, piece["dp"])
    return pl.multiple_of((shard * parts + part) * part_rows, 128)


def base_sum(place, rows, total, buffers, pieces, sizes):
    for piece in pieces:
        columns = pl.ds(column_of(place, piece, *sizes), piece["rows"])
        part = pl.ds(piece["first"], piece["rows"])
        left = jnp.concatenate([ref[:, columns] for ref in rows], axis=0) if len(rows) > 1 else rows[0][:, columns]
        value = jnp.dot(left, buffers[piece["buffer"]][part, :], preferred_element_type=F32)
        total = value if total is None else total + value
    return total


def base_kernel(pieces, alone, sizes, tokens, tokens_pair, before, before_pair, *refs):
    place = position()
    buffers, (total, total_pair) = refs[:-2], refs[-2:]
    count = tokens.shape[0]
    both = base_sum(place, (tokens, tokens_pair), None, buffers, alone, sizes)
    total[...] = base_sum(place, (tokens,), before[...] + both[:count], buffers, pieces, sizes)
    total_pair[...] = before_pair[...] + both[count:]


def middle_kernel(parts, told, *refs):
    place = position()
    (tokens, own, received, cotangent, gain, low_rank, up), refs = refs[:7], refs[7:]
    (keys, pre_low, low_grad), grads, (held, copied) = refs[:3], refs[3:-2], refs[-2:]
    projected = own[...] + received[...]
    rows, width = projected.shape
    gains = gain[...]
    slots, counts = told[:, :1], told[:, 1:2]
    adapter_total = jnp.sum(jnp.where(slots == slots[:1], counts, 0.0), axis=0, keepdims=True)
    live = lax.broadcasted_iota(jnp.int32, (rows, 1), 0).astype(F32) < counts[:1]
    weight = rows / jnp.broadcast_to(adapter_total, (rows, 1))
    weight = jnp.where(live, weight, 0.0)
    heads = []
    for head in range(width // HD):
        columns = slice(head * HD, (head + 1) * HD)
        values = projected[:, columns]
        inverse = lax.rsqrt(jnp.mean(values * values, axis=-1, keepdims=True) + norm_eps)
        normed = values * inverse
        held[:, columns] = (normed * gains).astype(BF16)
        scaled = cotangent[:, columns].astype(F32) * weight * gains
        along = jnp.mean(scaled * normed, axis=-1, keepdims=True)
        heads.append(inverse * (scaled - normed * along))
    copy = pltpu.make_async_copy(held, keys, copied)
    copy.start()
    pre = jnp.concatenate(heads, axis=-1)
    pre_low[...] = pre.astype(BF16)
    (pre_high, pre_rest), (up_high, up_rest), (low_high, low_rest) = map(split_two, (pre, up[...], low_rank[...]))
    rank = up.shape[0]
    both = lax.dot_general(
        jnp.concatenate([pre_high, pre_rest], axis=0),
        jnp.concatenate([up_high, up_rest], axis=0),
        (((1,), (1,)), ((), ())),
        preferred_element_type=F32,
    )
    grad = adapter_scale * (both[:rows, :rank] + both[:rows, rank:] + both[rows:, :rank])
    low_grad[...] = grad
    across = (((0,), (0,)), ((), ()))
    both = lax.dot_general(
        jnp.concatenate([low_high, low_rest], axis=-1), pre_high, across, preferred_element_type=F32
    )
    rest = lax.dot_general(low_high, pre_rest, across, preferred_element_type=F32)
    up_grad = adapter_scale * (both[:rank] + both[rank:] + rest)
    split = jnp.concatenate(split_two(grad), axis=-1)
    down_width, up_width = tokens.shape[1] // parts, width // parts
    for partner, out in enumerate(grads):
        part = place[0] ^ partner
        columns = pl.ds(pl.multiple_of(part * down_width, 128), down_width)
        both = lax.dot_general(split, tokens[:, columns], (((0,), (0,)), ((), ())), preferred_element_type=F32)
        out[:, :down_width] = (both[:rank] + both[rank:]).astype(out.dtype)
        for other in range(parts):

            @pl.when(part == other)
            def _():
                out[:, down_width:] = up_grad[:, other * up_width : (other + 1) * up_width].astype(out.dtype)
    copy.wait()


def input_grad_kernel(pieces, sizes, pre_low, low_grad, split, *refs):
    place = position()
    buffers, (out, held, copied) = refs[:-3], refs[-3:]
    rank = low_grad.shape[1]
    high, low = split_two(low_grad[...])
    left = jnp.concatenate([high, high, low], axis=-1)
    turned = pre_low[...].T
    copies = []
    for index, piece in enumerate(pieces):
        if index == 0 or piece["buffer"] != pieces[index - 1]["buffer"]:
            whole = jnp.dot(buffers[piece["buffer"]][...], turned, preferred_element_type=F32).T
        columns = pl.ds(column_of(place, piece, *sizes), piece["rows"])
        value = whole[:, piece["first"] : piece["first"] + piece["rows"]]
        value = value + jnp.dot(left, split[:, columns], preferred_element_type=F32)
        held[:, columns] = value.astype(BF16)
        copies.append(pltpu.make_async_copy(held.at[:, columns], out.at[:, columns], copied.at[index]))
        copies[-1].start()
    for copy in copies:
        copy.wait()


def sum_kernel(told, *refs):
    grads, (down, up, down_held, up_held, copied) = refs[:-5], refs[-5:]
    width = down.shape[2]
    copies = []
    for stored in range(down.shape[0]):
        total = jnp.zeros(grads[0].shape, F32)
        for partner, grad in enumerate(grads):
            slot = told[partner : partner + 1, :1]
            total = total + jnp.where(slot == stored, grad[...].astype(F32), 0.0)
        down_held[stored] = total[:, :width]
        up_held[stored] = total[:, width:]
        for source, target in ((down_held, down), (up_held, up)):
            copies.append(pltpu.make_async_copy(source.at[stored], target.at[stored], copied.at[len(copies)]))
            copies[-1].start()
    for copy in copies:
        copy.wait()


def ordered(value, *earlier):
    return lax.optimization_barrier((value, *earlier))[0]


def flip(value, axis, size, bits):
    return lax.ppermute(value, axis, [(i, i ^ bits) for i in range(size)])


def on_device_lines(
    sizes,
    tokens,
    frozen_key_matrix,
    adapter_down_factor,
    adapter_up_factor,
    key_norm_gain,
    adapter_offset,
    loss_row_count,
    cotangent,
):
    parts, shards = sizes
    rows, model_width = tokens.shape
    key_width = frozen_key_matrix.shape[1]
    stored, down_width, rank = adapter_down_factor.shape
    up_width = adapter_up_factor.shape[2]
    shard_rows = frozen_key_matrix.shape[0]
    part_rows = shard_rows // parts
    over_dp = lambda value, bits: flip(value, "dp", parts, bits)
    over_z = lambda value, bits: flip(value, "fsdp", shards, bits * CORES)
    over_core = lambda value: flip(value, "fsdp", shards, 1)

    def over_split(value, dp_bits, z_bits):
        pairs = []
        for i in range(parts):
            for j in range(shards):
                core = j % CORES
                pairs.append((i * shards + j, (i ^ dp_bits[core]) * shards + (j ^ (z_bits[core] * CORES))))
        return lax.ppermute(value, ("dp", "fsdp"), pairs)

    near_both = (CORES * part_rows, key_width)

    def joined(*values):
        rows = len(values) * part_rows
        outs = [((rows, key_width), BF16)]
        return call(functools.partial(join_kernel, part_rows), outs, [(vmem, value) for value in values], "join")[0]

    matrix = frozen_key_matrix
    part = ((part_rows, key_width), BF16)
    near = lax.dynamic_slice_in_dim(matrix, lax.axis_index("dp") * part_rows, part_rows, 0)
    z1, z2 = over_z(near, 1), over_z(near, 2)
    (info,) = call(info_kernel, [((1, HD), F32)], [(vmem, adapter_offset)], "info")
    offsets = [info] + [over_dp(info, bits) for bits in range(1, parts)]
    held = call(
        hold_kernel,
        [((1, HD), F32), ((stored, rank, down_width), F32), (adapter_up_factor.shape, F32)],
        [(vmem, loss_row_count), (vmem, jnp.swapaxes(adapter_down_factor, 1, 2)), (vmem, adapter_up_factor)],
        "hold",
    )
    offsets, held = lax.optimization_barrier((offsets, held))
    wide = down_width + up_width + HD
    slots, own, sooner, later = call(
        messages_kernel,
        [((parts, HD), F32), ((rank, wide), F32), ((2 * rank, wide), F32), ((rank, wide), F32)],
        [(vmem, value) for value in (*offsets, *held)],
        "adapter_messages",
    )
    z1, z2 = ordered((z1, z2), sooner)
    sooner = over_split(sooner, (1, 2), (0, 0))
    z3 = over_z(z2, 1)
    z1_pair, z2_pair, sooner = lax.optimization_barrier((over_core(z1), over_core(z2), sooner))
    m12 = joined(z1, z1_pair, z2, z2_pair)
    xy12 = over_split(m12, (1, 2), (0, 0))
    matrix_pair, tokens_pair = over_core(ordered(matrix, m12)), over_core(ordered(tokens, m12))
    z3, matrix_pair, tokens_pair = lax.optimization_barrier((z3, matrix_pair, tokens_pair))
    (onward,) = call(pass_on_kernel, [((2 * rank, wide), F32)], [(vmem, later), (vmem, sooner)], "pass_on")
    later = over_split(onward, (2, 1), (0, 0))
    m3 = joined(z3, over_core(z3))
    xy3 = over_split(m3, (1, 2), (0, 0))
    (fars,) = call(
        functools.partial(part_kernel, parts - 1), [(near_both, BF16)], [(vmem, matrix), (vmem, matrix_pair)], "far"
    )
    d13 = over_split(ordered(fars, z3), (0, 0), (1, 3))
    xy12 = ordered(xy12, m3)
    (m4,) = call(functools.partial(take_kernel, part_rows, (2,)), [part], [(vmem, xy12)], "take")
    xy4 = over_split(m4, (2, 1), (0, 0))

    def piece(z, dp_bits, core, count=part_rows, first=0):
        pair = lambda value: value if isinstance(value, tuple) else (value, value)
        dp_bits = None if dp_bits is None else pair(dp_bits)
        return dict(z=pair(z), dp=dp_bits, core=core, rows=count, first=first)

    def two(z, dp_bits, core=0, first=0):
        return [piece(z, dp_bits, core, first=first), piece(z, dp_bits, 1 - core, first=first + part_rows)]

    def flat(batch):
        buffers = [value for value, _ in batch]
        pieces = [dict(item, buffer=index) for index, (_, items) in enumerate(batch) for item in items]
        return buffers, pieces

    def base(before, shared, alone):
        buffers, pieces = flat(shared + alone)
        mine = [item for item in pieces if item["buffer"] < len(shared)]
        lone = [item for item in pieces if item["buffer"] >= len(shared)]
        return call(
            functools.partial(base_kernel, mine, lone, (part_rows, parts)),
            [((rows, key_width), F32)] * 2,
            [(vmem, value) for value in (tokens, tokens_pair, *before, *buffers)],
            "base",
        )

    split, up, low_rank, total, told = call(
        low_rank_kernel,
        [
            ((3 * rank, model_width), BF16),
            ((rank, key_width), F32),
            ((rows, rank), F32),
            ((rows, key_width), F32),
            ((parts, HD), F32),
        ],
        [(vmem, value) for value in (tokens, slots, own, sooner, later)],
        "low_rank",
        moved=12 * 2**20,
    )
    last = CORES * part_rows
    shared = [
        (matrix, [piece(0, None, 0, shard_rows)]),
        (matrix_pair, [piece(0, None, 1, shard_rows)]),
        (m12, two(1, 0) + two(2, 0, 0, last)),
        (m3, two(3, 0)),
    ]
    early = [(xy12, two(1, (1, 2)) + two(2, (1, 2), 0, last))]
    totals = base((total, jnp.zeros_like(total)), shared, early)
    xy12, xy3, xy4, d13, totals = lax.optimization_barrier((xy12, xy3, xy4, d13, totals))
    late = [(xy3, two(3, (1, 2))), (d13, two((1, 3), 3)), (xy4, [piece(2, 3, 0)])]
    total, total_pair = base(totals, [], late)
    received = over_core(total_pair)
    (lone,) = call(
        functools.partial(join_kernel, None),
        [((9 * part_rows, key_width), BF16)],
        [(vmem, value) for value in (xy12, xy3, d13, xy4)],
        "join",
    )
    lone_pair = over_core(ordered(lone, received))
    keys, pre_low, low_grad, *grads = call(
        functools.partial(middle_kernel, parts),
        [((rows, key_width), BF16), ((rows, key_width), BF16), ((rows, rank), F32)]
        + [((rank, down_width + up_width), F32)]
        + [((rank, down_width + up_width), BF16)] * (parts - 1),
        [
            (vmem, value)
            for value in (told, tokens, total, received, cotangent, key_norm_gain.reshape(1, HD), low_rank, up)
        ],
        "key_norm",
        out=[hbm] + [vmem] * (2 + parts),
        scratch=[pltpu.VMEM((rows, key_width), BF16), pltpu.SemaphoreType.DMA],
    )
    others = two(1, (2, 1), 1) + two(2, (2, 1), 1, last) + two(3, (2, 1), 1, 2 * last) + two((3, 1), 3, 1, 3 * last)
    others = [(lone_pair, others + [piece(2, 3, 1, first=4 * last)])]
    received = [grads[0]] + [over_dp(grads[bits], bits) for bits in range(1, parts)]
    buffers, pieces = flat(shared + early + late + others)
    (input_grad,) = call(
        functools.partial(input_grad_kernel, pieces, (part_rows, parts)),
        [((rows, model_width), BF16)],
        [(vmem, pre_low), (vmem, low_grad), (vmem, split)] + [(vmem, value) for value in buffers],
        "input_grad",
        out=hbm,
        scratch=[pltpu.VMEM((rows, model_width), BF16), pltpu.SemaphoreType.DMA((len(pieces),))],
    )
    received, input_grad = lax.optimization_barrier((received, input_grad))
    down_sum, up_sum = call(
        sum_kernel,
        [((stored, rank, down_width), F32), ((stored, rank, up_width), F32)],
        [(vmem, told)] + [(vmem, value) for value in received],
        "grad_sum",
        out=hbm,
        scratch=[
            pltpu.VMEM((stored, rank, down_width), F32),
            pltpu.VMEM((stored, rank, up_width), F32),
            pltpu.SemaphoreType.DMA((2 * stored,)),
        ],
    )
    return keys, input_grad, jnp.swapaxes(down_sum, 1, 2), up_sum


def on_device_any(
    tokens,
    frozen_key_matrix,
    adapter_down_factor,
    adapter_up_factor,
    key_norm_gain,
    adapter_offset,
    loss_row_count,
    cotangent,
):
    row_count = tokens.shape[0]
    key_width = frozen_key_matrix.shape[1]
    stored_values = adapter_down_factor.shape[0]
    slot_value = adapter_offset[0, 0]
    live_count = loss_row_count[0, 0]
    selector = jnp.arange(stored_values, dtype=jnp.int32) == slot_value
    counted = jnp.where(selector, live_count, 0)
    summed_rows = lax.psum(counted, "dp")
    adapter_total = jnp.sum(jnp.where(selector, summed_rows, 0)).astype(F32)
    down_whole = lax.all_gather(adapter_down_factor, "dp", axis=1, tiled=True)
    up_whole = lax.all_gather(adapter_up_factor, "dp", axis=2, tiled=True)
    down_projection = lax.dynamic_index_in_dim(down_whole, slot_value, 0, keepdims=False)
    up_projection = lax.dynamic_index_in_dim(up_whole, slot_value, 0, keepdims=False)
    weight = lax.all_gather(frozen_key_matrix, "fsdp", axis=0, tiled=True)
    frozen_output = jnp.dot(tokens, weight, preferred_element_type=F32)
    tokens_float = tokens.astype(F32)
    lowrank_output = jnp.dot(tokens_float, down_projection, precision=HIGHEST)
    projected_keys = frozen_output + adapter_scale * jnp.dot(lowrank_output, up_projection, precision=HIGHEST)
    shaped = projected_keys.reshape(row_count, -1, HD)
    mean_square = jnp.mean(shaped * shaped, axis=-1, keepdims=True)
    inverse_rms = lax.rsqrt(mean_square + norm_eps)
    normed = shaped * inverse_rms
    keys = (normed * key_norm_gain).reshape(row_count, key_width).astype(BF16)
    row_mask = (jnp.arange(row_count, dtype=jnp.int32) < live_count).astype(F32)
    row_grad = cotangent.astype(F32) * row_mask[:, None] * (row_count / adapter_total)
    scaled_grad = row_grad.reshape(normed.shape) * key_norm_gain
    along_norm = jnp.mean(scaled_grad * normed, axis=-1, keepdims=True)
    prenorm_gradient = (inverse_rms * (scaled_grad - normed * along_norm)).reshape(row_count, key_width)
    pre_grad_low = prenorm_gradient.astype(BF16)
    lowrank_gradient = adapter_scale * jnp.dot(prenorm_gradient, up_projection.T, precision=HIGHEST)
    input_base = lax.dot_general(pre_grad_low, weight, (((1,), (1,)), ((), ())), preferred_element_type=F32)
    input_grad = (input_base + jnp.dot(lowrank_gradient, down_projection.T, precision=HIGHEST)).astype(BF16)
    down_grad = lax.dot_general(tokens_float, lowrank_gradient, (((0,), (0,)), ((), ())), precision=HIGHEST)
    up_factor_gradient = adapter_scale * lax.dot_general(
        lowrank_output, prenorm_gradient, (((0,), (0,)), ((), ())), precision=HIGHEST
    )
    selector_float = selector.astype(F32)
    down_terms = selector_float[:, None, None] * down_grad[None]
    up_terms = selector_float[:, None, None] * up_factor_gradient[None]
    down_sum = lax.psum_scatter(down_terms, "dp", scatter_dimension=1, tiled=True)
    up_sum = lax.psum_scatter(up_terms, "dp", scatter_dimension=2, tiled=True)
    return keys, input_grad, down_sum, up_sum


def solution(mesh):
    placed = (
        P(("dp", "fsdp"), None),
        P("fsdp", None),
        P("fsdp", "dp", None),
        P("fsdp", None, "dp"),
        P(),
        P("dp", "fsdp"),
        P("dp", "fsdp"),
        P(("dp", "fsdp"), None),
    )
    sizes = mesh.shape["dp"], mesh.shape["fsdp"]
    lines = sizes == (4, 4 * CORES)
    return jax.shard_map(
        functools.partial(on_device_lines, sizes) if lines else on_device_any,
        mesh=mesh,
        in_specs=placed,
        out_specs=(
            P(("dp", "fsdp"), None),
            P(("dp", "fsdp"), None),
            P("fsdp", "dp", None),
            P("fsdp", None, "dp"),
        ),
        check_vma=False,
    )
```

```python
import functools

import jax
import jax.numpy as jnp
from jax import lax
from jax.experimental import pallas as pl
from jax.experimental.pallas import tpu as pltpu
from jax.sharding import PartitionSpec as P

HD = 128
CORES = 2

adapter_scale = 2.0
norm_eps = 1e-06

F32 = jnp.float32
BF16 = jnp.bfloat16
HIGHEST = lax.Precision.HIGHEST
VMEM_LIMIT = 8 * 2**20

vmem = pl.BlockSpec(memory_space=pltpu.VMEM)
smem = pl.BlockSpec(memory_space=pltpu.SMEM)
hbm = pl.BlockSpec(memory_space=pltpu.HBM)


def split_two(value):
    high = value.astype(BF16)
    low = (value - high.astype(F32)).astype(BF16)
    return high, low


def call(kernel, outs, ins, name, moved=0, out=vmem, scratch=()):
    return pl.pallas_call(
        kernel,
        out_shape=[jax.ShapeDtypeStruct(shape, dtype) for shape, dtype in outs],
        in_specs=[spec for spec, _ in ins],
        out_specs=out if isinstance(out, list) else [out] * len(outs),
        scratch_shapes=scratch,
        compiler_params=pltpu.CompilerParams(vmem_limit_bytes=VMEM_LIMIT),
        cost_estimate=pl.CostEstimate(flops=0, bytes_accessed=moved, transcendentals=0),
        name=name,
    )(*[value for _, value in ins])


def position():
    fsdp = lax.axis_index("fsdp")
    return lax.axis_index("dp"), lax.div(fsdp, CORES), lax.rem(fsdp, CORES)


def part_kernel(bits, *refs):
    out = refs[-1]
    rows = out.shape[0] // (len(refs) - 1)
    part = lax.axis_index("dp") ^ bits
    for index, matrix in enumerate(refs[:-1]):
        out[index * rows : (index + 1) * rows] = matrix[pl.ds(pl.multiple_of(part * rows, rows), rows), :]


def info_kernel(offset, info):
    info[...] = jnp.broadcast_to(offset[...].astype(F32), info.shape)


def hold_kernel(count, down, up, count_held, down_held, up_held):
    count_held[...] = jnp.broadcast_to(count[...].astype(F32), count_held.shape)
    down_held[...] = down[...]
    up_held[...] = up[...]


def chosen(stored, slot):
    return sum(jnp.where(slot == index, stored[index], 0.0) for index in range(stored.shape[0]))


def messages_kernel(*refs):
    parts = len(refs) - 7
    offsets, (count, down, up), (slots, own, sooner, later) = refs[:parts], refs[parts : parts + 3], refs[parts + 3 :]
    rank, width = down.shape[1], down.shape[2]
    wide = width + up.shape[2]
    first_core = position()[2] == 0
    for partner, offset in enumerate(offsets):
        slots[partner : partner + 1, :] = offset[...]
    near, side, beside, far = (offset[:, :1] for offset in offsets)
    wanted = jnp.where(first_core, side, beside), jnp.where(first_core, beside, side)
    for slot, out, first in ((near, own, 0), (wanted[0], sooner, 0), (wanted[1], later, 0), (far, sooner, rank)):
        rows = pl.ds(first, rank)
        out[rows, :width] = chosen(down, slot)
        out[rows, width:wide] = chosen(up, slot)
        out[rows, wide:] = jnp.broadcast_to(count[...], (rank, HD))


def pass_on_kernel(later, received, out):
    rank = later.shape[0]
    out[:rank] = later[...]
    out[rank:] = received[rank:]


def take_kernel(each, wanted, value, out):
    for index, place in enumerate(wanted):
        out[index * each : (index + 1) * each] = value[place * each : (place + 1) * each]


def join_kernel(each, *refs):
    out, first = refs[-1], 0
    for ref in refs[:-1]:
        rows = each or ref.shape[0]
        out[first : first + rows] = ref[:rows]
        first += rows


def low_rank_kernel(tokens, slots, own, sooner, later, split, up, low_rank, total, told):
    rank = low_rank.shape[1]
    messages = own, sooner.at[:rank], later.at[:rank], later.at[rank:]
    parts = len(messages)
    down_width = tokens.shape[1] // parts
    up_width = up.shape[1] // parts
    dp, _, core = position()
    lane = lax.broadcasted_iota(jnp.int32, (1, HD), 1)
    counts = [message[:1, down_width + up_width :] for message in messages]
    counts[1:3] = jnp.where(core == 0, counts[1], counts[2]), jnp.where(core == 0, counts[2], counts[1])
    for partner, count in enumerate(counts):
        told[partner : partner + 1, :] = jnp.where(lane == 0, slots[partner : partner + 1, :], count)
    partners = 0, jnp.where(core == 0, 1, 2), jnp.where(core == 0, 2, 1), 3
    for partner, message in zip(partners, messages):
        part = dp ^ partner
        columns = pl.ds(pl.multiple_of(part * down_width, 128), down_width)
        high, low = split_two(message[:, :down_width])
        split[:rank, columns] = high
        split[rank : 2 * rank, columns] = low
        split[2 * rank :, columns] = high
        columns = pl.ds(pl.multiple_of(part * up_width, 128), up_width)
        up[:, columns] = message[:, down_width : down_width + up_width]
    both = lax.dot_general(
        tokens[...], split[: 2 * rank, :], (((1,), (1,)), ((), ())), preferred_element_type=F32
    )
    low_rank[...] = both[:, :rank] + both[:, rank:]
    total[...] = adapter_scale * jnp.dot(low_rank[...], up[...], precision=HIGHEST, preferred_element_type=F32)


def by_core(place, value):
    first, second = value
    return first if first == second else jnp.where(place[2] == 0, first, second)


def column_of(place, piece, part_rows, parts):
    shard = (place[1] ^ by_core(place, piece["z"])) * CORES + (place[2] ^ piece["core"])
    part = 0 if piece["dp"] is None else place[0] ^ by_core(place, piece["dp"])
    return pl.multiple_of((shard * parts + part) * part_rows, 128)


def base_sum(place, rows, total, buffers, pieces, sizes):
    for piece in pieces:
        columns = pl.ds(column_of(place, piece, *sizes), piece["rows"])
        part = pl.ds(piece["first"], piece["rows"])
        left = jnp.concatenate([ref[:, columns] for ref in rows], axis=0) if len(rows) > 1 else rows[0][:, columns]
        value = jnp.dot(left, buffers[piece["buffer"]][part, :], preferred_element_type=F32)
        total = value if total is None else total + value
    return total


def base_kernel(pieces, alone, sizes, tokens, tokens_pair, before, before_pair, *refs):
    place = position()
    buffers, (total, total_pair) = refs[:-2], refs[-2:]
    count = tokens.shape[0]
    both = base_sum(place, (tokens, tokens_pair), None, buffers, alone, sizes)
    total[...] = base_sum(place, (tokens,), before[...] + both[:count], buffers, pieces, sizes)
    total_pair[...] = before_pair[...] + both[count:]


def middle_kernel(parts, told, *refs):
    place = position()
    (tokens, own, received, cotangent, gain, low_rank, up), refs = refs[:7], refs[7:]
    (keys, pre_low, low_grad), grads, (held, copied) = refs[:3], refs[3:-2], refs[-2:]
    projected = own[...] + received[...]
    rows, width = projected.shape
    gains = gain[...]
    slots, counts = told[:, :1], told[:, 1:2]
    adapter_total = jnp.sum(jnp.where(slots == slots[:1], counts, 0.0), axis=0, keepdims=True)
    live = lax.broadcasted_iota(jnp.int32, (rows, 1), 0).astype(F32) < counts[:1]
    weight = rows / jnp.broadcast_to(adapter_total, (rows, 1))
    weight = jnp.where(live, weight, 0.0)
    heads = []
    for head in range(width // HD):
        columns = slice(head * HD, (head + 1) * HD)
        values = projected[:, columns]
        inverse = lax.rsqrt(jnp.mean(values * values, axis=-1, keepdims=True) + norm_eps)
        normed = values * inverse
        held[:, columns] = (normed * gains).astype(BF16)
        scaled = cotangent[:, columns].astype(F32) * weight * gains
        along = jnp.mean(scaled * normed, axis=-1, keepdims=True)
        heads.append(inverse * (scaled - normed * along))
    copy = pltpu.make_async_copy(held, keys, copied)
    copy.start()
    pre = jnp.concatenate(heads, axis=-1)
    pre_low[...] = pre.astype(BF16)
    (pre_high, pre_rest), (up_high, up_rest), (low_high, low_rest) = map(split_two, (pre, up[...], low_rank[...]))
    rank = up.shape[0]
    both = lax.dot_general(
        jnp.concatenate([pre_high, pre_rest], axis=0),
        jnp.concatenate([up_high, up_rest], axis=0),
        (((1,), (1,)), ((), ())),
        preferred_element_type=F32,
    )
    grad = adapter_scale * (both[:rows, :rank] + both[:rows, rank:] + both[rows:, :rank])
    low_grad[...] = grad
    across = (((0,), (0,)), ((), ()))
    both = lax.dot_general(
        jnp.concatenate([low_high, low_rest], axis=-1), pre_high, across, preferred_element_type=F32
    )
    rest = lax.dot_general(low_high, pre_rest, across, preferred_element_type=F32)
    up_grad = adapter_scale * (both[:rank] + both[rank:] + rest)
    split = jnp.concatenate(split_two(grad), axis=-1)
    down_width, up_width = tokens.shape[1] // parts, width // parts
    for partner, out in enumerate(grads):
        part = place[0] ^ partner
        columns = pl.ds(pl.multiple_of(part * down_width, 128), down_width)
        both = lax.dot_general(split, tokens[:, columns], (((0,), (0,)), ((), ())), preferred_element_type=F32)
        out[:, :down_width] = (both[:rank] + both[rank:]).astype(out.dtype)
        for other in range(parts):

            @pl.when(part == other)
            def _():
                out[:, down_width:] = up_grad[:, other * up_width : (other + 1) * up_width].astype(out.dtype)
    copy.wait()


def input_grad_kernel(pieces, sizes, pre_low, low_grad, split, *refs):
    place = position()
    buffers, (out, held, copied) = refs[:-3], refs[-3:]
    rank = low_grad.shape[1]
    high, low = split_two(low_grad[...])
    left = jnp.concatenate([high, high, low], axis=-1)
    turned = pre_low[...].T
    copies = []
    for index, piece in enumerate(pieces):
        if index == 0 or piece["buffer"] != pieces[index - 1]["buffer"]:
            whole = jnp.dot(buffers[piece["buffer"]][...], turned, preferred_element_type=F32).T
        columns = pl.ds(column_of(place, piece, *sizes), piece["rows"])
        value = whole[:, piece["first"] : piece["first"] + piece["rows"]]
        value = value + jnp.dot(left, split[:, columns], preferred_element_type=F32)
        held[:, columns] = value.astype(BF16)
        copies.append(pltpu.make_async_copy(held.at[:, columns], out.at[:, columns], copied.at[index]))
        copies[-1].start()
    for copy in copies:
        copy.wait()


def sum_kernel(told, *refs):
    grads, (down, up, down_held, up_held, copied) = refs[:-5], refs[-5:]
    width = down.shape[2]
    copies = []
    for stored in range(down.shape[0]):
        total = jnp.zeros(grads[0].shape, F32)
        for partner, grad in enumerate(grads):
            slot = told[partner : partner + 1, :1]
            total = total + jnp.where(slot == stored, grad[...].astype(F32), 0.0)
        down_held[stored] = total[:, :width]
        up_held[stored] = total[:, width:]
        for source, target in ((down_held, down), (up_held, up)):
            copies.append(pltpu.make_async_copy(source.at[stored], target.at[stored], copied.at[len(copies)]))
            copies[-1].start()
    for copy in copies:
        copy.wait()


def ordered(value, *earlier):
    return lax.optimization_barrier((value, *earlier))[0]


def flip(value, axis, size, bits):
    return lax.ppermute(value, axis, [(i, i ^ bits) for i in range(size)])


def on_device_lines(
    sizes,
    tokens,
    frozen_key_matrix,
    adapter_down_factor,
    adapter_up_factor,
    key_norm_gain,
    adapter_offset,
    loss_row_count,
    cotangent,
):
    parts, shards = sizes
    rows, model_width = tokens.shape
    key_width = frozen_key_matrix.shape[1]
    stored, down_width, rank = adapter_down_factor.shape
    up_width = adapter_up_factor.shape[2]
    shard_rows = frozen_key_matrix.shape[0]
    part_rows = shard_rows // parts
    over_dp = lambda value, bits: flip(value, "dp", parts, bits)
    over_z = lambda value, bits: flip(value, "fsdp", shards, bits * CORES)
    over_core = lambda value: flip(value, "fsdp", shards, 1)

    def over_split(value, dp_bits, z_bits):
        pairs = []
        for i in range(parts):
            for j in range(shards):
                core = j % CORES
                pairs.append((i * shards + j, (i ^ dp_bits[core]) * shards + (j ^ (z_bits[core] * CORES))))
        return lax.ppermute(value, ("dp", "fsdp"), pairs)

    near_both = (CORES * part_rows, key_width)

    def joined(*values):
        rows = len(values) * part_rows
        outs = [((rows, key_width), BF16)]
        return call(functools.partial(join_kernel, part_rows), outs, [(vmem, value) for value in values], "join")[0]

    matrix = frozen_key_matrix
    part = ((part_rows, key_width), BF16)
    near = lax.dynamic_slice_in_dim(matrix, lax.axis_index("dp") * part_rows, part_rows, 0)
    z1, z2 = over_z(near, 1), over_z(near, 2)
    (info,) = call(info_kernel, [((1, HD), F32)], [(vmem, adapter_offset)], "info")
    offsets = [info] + [over_dp(info, bits) for bits in range(1, parts)]
    held = call(
        hold_kernel,
        [((1, HD), F32), ((stored, rank, down_width), F32), (adapter_up_factor.shape, F32)],
        [(vmem, loss_row_count), (vmem, jnp.swapaxes(adapter_down_factor, 1, 2)), (vmem, adapter_up_factor)],
        "hold",
    )
    offsets, held = lax.optimization_barrier((offsets, held))
    wide = down_width + up_width + HD
    slots, own, sooner, later = call(
        messages_kernel,
        [((parts, HD), F32), ((rank, wide), F32), ((2 * rank, wide), F32), ((rank, wide), F32)],
        [(vmem, value) for value in (*offsets, *held)],
        "adapter_messages",
    )
    z1, z2 = ordered((z1, z2), sooner)
    sooner = over_split(sooner, (1, 2), (0, 0))
    z3 = over_z(z2, 1)
    z1_pair, z2_pair, sooner = lax.optimization_barrier((over_core(z1), over_core(z2), sooner))
    m12 = joined(z1, z1_pair, z2, z2_pair)
    xy12 = over_split(m12, (1, 2), (0, 0))
    matrix_pair, tokens_pair = over_core(ordered(matrix, m12)), over_core(ordered(tokens, m12))
    z3, matrix_pair, tokens_pair = lax.optimization_barrier((z3, matrix_pair, tokens_pair))
    (onward,) = call(pass_on_kernel, [((2 * rank, wide), F32)], [(vmem, later), (vmem, sooner)], "pass_on")
    later = over_split(onward, (2, 1), (0, 0))
    m3 = joined(z3, over_core(z3))
    xy3 = over_split(m3, (1, 2), (0, 0))
    (fars,) = call(
        functools.partial(part_kernel, parts - 1), [(near_both, BF16)], [(vmem, matrix), (vmem, matrix_pair)], "far"
    )
    d13 = over_split(ordered(fars, z3), (0, 0), (1, 3))
    xy12 = ordered(xy12, m3)
    (m4,) = call(functools.partial(take_kernel, part_rows, (2,)), [part], [(vmem, xy12)], "take")
    xy4 = over_split(m4, (2, 1), (0, 0))

    def piece(z, dp_bits, core, count=part_rows, first=0):
        pair = lambda value: value if isinstance(value, tuple) else (value, value)
        dp_bits = None if dp_bits is None else pair(dp_bits)
        return dict(z=pair(z), dp=dp_bits, core=core, rows=count, first=first)

    def two(z, dp_bits, core=0, first=0):
        return [piece(z, dp_bits, core, first=first), piece(z, dp_bits, 1 - core, first=first + part_rows)]

    def flat(batch):
        buffers = [value for value, _ in batch]
        pieces = [dict(item, buffer=index) for index, (_, items) in enumerate(batch) for item in items]
        return buffers, pieces

    def base(before, shared, alone):
        buffers, pieces = flat(shared + alone)
        mine = [item for item in pieces if item["buffer"] < len(shared)]
        lone = [item for item in pieces if item["buffer"] >= len(shared)]
        return call(
            functools.partial(base_kernel, mine, lone, (part_rows, parts)),
            [((rows, key_width), F32)] * 2,
            [(vmem, value) for value in (tokens, tokens_pair, *before, *buffers)],
            "base",
        )

    split, up, low_rank, total, told = call(
        low_rank_kernel,
        [
            ((3 * rank, model_width), BF16),
            ((rank, key_width), F32),
            ((rows, rank), F32),
            ((rows, key_width), F32),
            ((parts, HD), F32),
        ],
        [(vmem, value) for value in (tokens, slots, own, sooner, later)],
        "low_rank",
        moved=12 * 2**20,
    )
    last = CORES * part_rows
    shared = [
        (matrix, [piece(0, None, 0, shard_rows)]),
        (matrix_pair, [piece(0, None, 1, shard_rows)]),
        (m12, two(1, 0) + two(2, 0, 0, last)),
        (m3, two(3, 0)),
    ]
    early = [(xy12, two(1, (1, 2)) + two(2, (1, 2), 0, last))]
    totals = base((total, jnp.zeros_like(total)), shared, early)
    xy12, xy3, xy4, d13, totals = lax.optimization_barrier((xy12, xy3, xy4, d13, totals))
    late = [(xy3, two(3, (1, 2))), (d13, two((1, 3), 3)), (xy4, [piece(2, 3, 0)])]
    total, total_pair = base(totals, [], late)
    received = over_core(total_pair)
    (lone,) = call(
        functools.partial(join_kernel, None),
        [((9 * part_rows, key_width), BF16)],
        [(vmem, value) for value in (xy12, xy3, d13, xy4)],
        "join",
    )
    lone_pair = over_core(ordered(lone, received))
    keys, pre_low, low_grad, *grads = call(
        functools.partial(middle_kernel, parts),
        [((rows, key_width), BF16), ((rows, key_width), BF16), ((rows, rank), F32)]
        + [((rank, down_width + up_width), F32)]
        + [((rank, down_width + up_width), BF16)] * (parts - 1),
        [
            (vmem, value)
            for value in (told, tokens, total, received, cotangent, key_norm_gain.reshape(1, HD), low_rank, up)
        ],
        "key_norm",
        out=[hbm] + [vmem] * (2 + parts),
        scratch=[pltpu.VMEM((rows, key_width), BF16), pltpu.SemaphoreType.DMA],
    )
    others = two(1, (2, 1), 1) + two(2, (2, 1), 1, last) + two(3, (2, 1), 1, 2 * last) + two((3, 1), 3, 1, 3 * last)
    others = [(lone_pair, others + [piece(2, 3, 1, first=4 * last)])]
    received = [grads[0]] + [over_dp(grads[bits], bits) for bits in range(1, parts)]
    buffers, pieces = flat(shared + others + early + late)
    (input_grad,) = call(
        functools.partial(input_grad_kernel, pieces, (part_rows, parts)),
        [((rows, model_width), BF16)],
        [(vmem, pre_low), (vmem, low_grad), (vmem, split)] + [(vmem, value) for value in buffers],
        "input_grad",
        out=hbm,
        scratch=[pltpu.VMEM((rows, model_width), BF16), pltpu.SemaphoreType.DMA((len(pieces),))],
    )
    received, input_grad = lax.optimization_barrier((received, input_grad))
    down_sum, up_sum = call(
        sum_kernel,
        [((stored, rank, down_width), F32), ((stored, rank, up_width), F32)],
        [(vmem, told)] + [(vmem, value) for value in received],
        "grad_sum",
        out=hbm,
        scratch=[
            pltpu.VMEM((stored, rank, down_width), F32),
            pltpu.VMEM((stored, rank, up_width), F32),
            pltpu.SemaphoreType.DMA((2 * stored,)),
        ],
    )
    return keys, input_grad, jnp.swapaxes(down_sum, 1, 2), up_sum


def on_device_any(
    tokens,
    frozen_key_matrix,
    adapter_down_factor,
    adapter_up_factor,
    key_norm_gain,
    adapter_offset,
    loss_row_count,
    cotangent,
):
    row_count = tokens.shape[0]
    key_width = frozen_key_matrix.shape[1]
    stored_values = adapter_down_factor.shape[0]
    slot_value = adapter_offset[0, 0]
    live_count = loss_row_count[0, 0]
    selector = jnp.arange(stored_values, dtype=jnp.int32) == slot_value
    counted = jnp.where(selector, live_count, 0)
    summed_rows = lax.psum(counted, "dp")
    adapter_total = jnp.sum(jnp.where(selector, summed_rows, 0)).astype(F32)
    down_whole = lax.all_gather(adapter_down_factor, "dp", axis=1, tiled=True)
    up_whole = lax.all_gather(adapter_up_factor, "dp", axis=2, tiled=True)
    down_projection = lax.dynamic_index_in_dim(down_whole, slot_value, 0, keepdims=False)
    up_projection = lax.dynamic_index_in_dim(up_whole, slot_value, 0, keepdims=False)
    weight = lax.all_gather(frozen_key_matrix, "fsdp", axis=0, tiled=True)
    frozen_output = jnp.dot(tokens, weight, preferred_element_type=F32)
    tokens_float = tokens.astype(F32)
    lowrank_output = jnp.dot(tokens_float, down_projection, precision=HIGHEST)
    projected_keys = frozen_output + adapter_scale * jnp.dot(lowrank_output, up_projection, precision=HIGHEST)
    shaped = projected_keys.reshape(row_count, -1, HD)
    mean_square = jnp.mean(shaped * shaped, axis=-1, keepdims=True)
    inverse_rms = lax.rsqrt(mean_square + norm_eps)
    normed = shaped * inverse_rms
    keys = (normed * key_norm_gain).reshape(row_count, key_width).astype(BF16)
    row_mask = (jnp.arange(row_count, dtype=jnp.int32) < live_count).astype(F32)
    row_grad = cotangent.astype(F32) * row_mask[:, None] * (row_count / adapter_total)
    scaled_grad = row_grad.reshape(normed.shape) * key_norm_gain
    along_norm = jnp.mean(scaled_grad * normed, axis=-1, keepdims=True)
    prenorm_gradient = (inverse_rms * (scaled_grad - normed * along_norm)).reshape(row_count, key_width)
    pre_grad_low = prenorm_gradient.astype(BF16)
    lowrank_gradient = adapter_scale * jnp.dot(prenorm_gradient, up_projection.T, precision=HIGHEST)
    input_base = lax.dot_general(pre_grad_low, weight, (((1,), (1,)), ((), ())), preferred_element_type=F32)
    input_grad = (input_base + jnp.dot(lowrank_gradient, down_projection.T, precision=HIGHEST)).astype(BF16)
    down_grad = lax.dot_general(tokens_float, lowrank_gradient, (((0,), (0,)), ((), ())), precision=HIGHEST)
    up_factor_gradient = adapter_scale * lax.dot_general(
        lowrank_output, prenorm_gradient, (((0,), (0,)), ((), ())), precision=HIGHEST
    )
    selector_float = selector.astype(F32)
    down_terms = selector_float[:, None, None] * down_grad[None]
    up_terms = selector_float[:, None, None] * up_factor_gradient[None]
    down_sum = lax.psum_scatter(down_terms, "dp", scatter_dimension=1, tiled=True)
    up_sum = lax.psum_scatter(up_terms, "dp", scatter_dimension=2, tiled=True)
    return keys, input_grad, down_sum, up_sum


def solution(mesh):
    placed = (
        P(("dp", "fsdp"), None),
        P("fsdp", None),
        P("fsdp", "dp", None),
        P("fsdp", None, "dp"),
        P(),
        P("dp", "fsdp"),
        P("dp", "fsdp"),
        P(("dp", "fsdp"), None),
    )
    sizes = mesh.shape["dp"], mesh.shape["fsdp"]
    lines = sizes == (4, 4 * CORES)
    return jax.shard_map(
        functools.partial(on_device_lines, sizes) if lines else on_device_any,
        mesh=mesh,
        in_specs=placed,
        out_specs=(
            P(("dp", "fsdp"), None),
            P(("dp", "fsdp"), None),
            P("fsdp", "dp", None),
            P("fsdp", None, "dp"),
        ),
        check_vma=False,
    )
```
